32 devices in a mesh: seq: 16 (over z, y, core), head: 2 (over x).
Axes of the slice: x: 2, y: 2, z: 4, core: 2. Of those that a mesh axis runs over, the one named last changes fastest.
Arguments:
- queries: bfloat16 [2048, 3072], P('seq', 'head'), may hold values from -6 to 6
- keys: bfloat16 [2048, 3072], P('seq', 'head'), may hold values from -6 to 6
- values: bfloat16 [2048, 3072], P('seq', 'head'), may hold values from -6 to 6
- cache_k: bfloat16 [2048, 3072], P('seq', 'head'), may hold values from -6 to 6
- cache_v: bfloat16 [2048, 3072], P('seq', 'head'), may hold values from -6 to 6
- sink_k: bfloat16 [8, 3072], P(None, 'head'), may hold values from -6 to 6
- sink_v: bfloat16 [8, 3072], P(None, 'head'), may hold values from -6 to 6
- suffix_lengths: int32 [4], replicated, may hold values from 1 to 1024, 2048 in all
- request_group: int32 [4], replicated, may hold values from 0 to 1
- w_out: bfloat16 [3072, 3072], P('head'), may hold values from -0.109375 to 0.109375
Outputs:
- projected: bfloat16 [3072, 2048], P('head', 'seq')
The draws below stay inside these ranges and needn't reach their ends.
All inputs are finite; a program needn't handle non-finite values.
Results may differ from the reference program's by a relative error of at most 0.011.
Values may be sent and summed in bfloat16 or wider, within the bound.
A program may use at most 128 MiB of HBM per device.

```python
import math
import jax
import jax.numpy as jnp
import numpy as np
from jax import lax

D = 3072
HEADS = 32
HD = 96
W = 1024
SINKS = 4
G = 2
HC = 3072
SUF = 2048
REQS = 4


def draw_queries(key, part):
    field = jnp.clip(jax.random.normal(jax.random.fold_in(key, 11), (SUF, HC), jnp.float32), -6.0, 6.0)
    return field.astype(jnp.bfloat16)


def draw_keys(key, part):
    field = jnp.clip(jax.random.normal(jax.random.fold_in(key, 13), (SUF, HC), jnp.float32), -6.0, 6.0)
    return field.astype(jnp.bfloat16)


def place_ends(values, own_key, least, top_value):
    longest = values.shape.index(max(values.shape))
    spots = []
    for shift in (0, 1):
        where = [jax.random.randint(jax.random.fold_in(own_key, axis), (), 0, length) for axis, length in enumerate(values.shape)]
        where[longest] = (where[longest] + shift) % values.shape[longest]
        spots.append(tuple(where))
    return values.at[spots[0]].set(least).at[spots[1]].set(top_value)


def shard_levels(key, extent, cuts, low, largest):
    def one(dim, shards_of):
        heights = jax.random.uniform(jax.random.fold_in(jax.random.fold_in(key, 6), dim), (shards_of,), jnp.float32, low / len(cuts), largest / len(cuts))
        return jnp.repeat(jnp.exp(heights), extent[dim] // shards_of).reshape((-1,) + (1,) * (len(extent) - dim - 1))

    gain = one(*cuts[0])
    for cut in cuts[1:]:
        gain = gain * one(*cut)
    return gain


def length_profile(count, total, reach, lean):
    portions = [(1 << 20) // math.isqrt(standing ** lean) + 1 for standing in range(2, count + 1)]
    spare, holding = total - reach - (count - 1), [1] * (count - 1)
    while spare > 0:
        candidates = [i for i in range(count - 1) if holding[i] < reach]
        pool, left = sum([portions[i] for i in candidates]), spare
        for i in candidates:
            addition = min(reach - holding[i], max(1, left * portions[i] // pool), spare)
            holding[i] = holding[i] + addition
            spare = spare - addition
    return np.array([reach] + holding)


def uneven_parts(key, number_of, total, most, skew):
    if number_of == 2:
        one = jax.random.randint(key, (), max(1, total - most), min(most, total - 1) + 1)
        return jnp.stack([one, total - one])
    tallies = jnp.asarray(length_profile(number_of, total, most, skew), jnp.int32)
    pairs = (number_of - 1) // 2
    giver, taker = tallies[1:1 + 2 * pairs:2], tallies[2:2 + 2 * pairs:2]
    room = jnp.minimum(giver - 1, most - taker)
    passed = jax.random.randint(jax.random.fold_in(key, 1), (pairs,), 0, 1 << 20) % (room + 1)
    tallies = tallies.at[1:1 + 2 * pairs:2].set(giver - passed).at[2:2 + 2 * pairs:2].set(taker + passed)
    return tallies[jax.random.permutation(jax.random.fold_in(key, 2), number_of)]


def noise(key, dims, width, most, split=(), kind=jnp.bfloat16):
    result = jax.random.normal(key, dims, jnp.float32) * width
    if len(split) > 0:
        result = shard_levels(key, dims, split, -0.22, 0.18) * result
    return jnp.clip(result, min=-most, max=most).astype(kind)


def setup_inputs(seed: int = 0) -> dict:
    seeds = jax.random.split(jax.random.key(seed), 11)
    return {
        "queries": draw_queries(jax.random.fold_in(seeds[10], 71), 0),
        "keys": draw_keys(jax.random.fold_in(seeds[10], 71), 0),
        "values": noise(seeds[2], (SUF, HC), 1.0, 6.0, ((0, 16), (1, 2))),
        "cache_k": noise(seeds[3], (G * W, HC), 1.0, 6.0, ((0, 16), (1, 2))),
        "cache_v": noise(seeds[4], (G * W, HC), 1.0, 6.0, ((0, 16), (1, 2))),
        "sink_k": noise(seeds[5], (G * SINKS, HC), 1.0, 6.0, ((1, 2),)),
        "sink_v": noise(seeds[6], (G * SINKS, HC), 1.0, 6.0, ((1, 2),)),
        "suffix_lengths": uneven_parts(seeds[7], REQS, SUF, W, 2).astype(jnp.int32),
        "request_group": place_ends(jax.random.randint(seeds[8], (REQS,), 0, G), jax.random.fold_in(seeds[8], 1), 0, G - 1).astype(jnp.int32),
        "w_out": noise(seeds[9], (HC, D), HC ** -0.5, 0.109375, ((0, 2),)),
    }


def describe(index, starts, lengths, groups):
    inside = (starts[None, :] <= index[:, None]) & (index[:, None] < (starts + lengths)[None, :])
    flag = inside.astype(jnp.int32)
    found = lax.optimization_barrier(jnp.sum(flag, axis=1))
    request = lax.optimization_barrier(jnp.sum(flag * jnp.arange(starts.shape[0], dtype=jnp.int32)[None, :], axis=1))
    request = jnp.where(found > 0, request, -1).astype(jnp.int32)
    offset = (index - lax.optimization_barrier(jnp.sum(flag * starts[None, :], axis=1))).astype(jnp.int32)
    group = lax.optimization_barrier(jnp.sum(flag * groups[None, :], axis=1)).astype(jnp.int32)
    return (request, offset, group)

def reference(queries, keys, values, cache_k, cache_v, sink_k, sink_v, suffix_lengths, request_group, w_out):
    block = math.gcd(512, SUF)
    starts = (jnp.cumsum(suffix_lengths) - suffix_lengths).astype(jnp.int32)
    scale = 1.0 / math.sqrt(HD)
    zeros = jnp.zeros((W, HC), keys.dtype)
    keys_pad = jnp.concatenate([zeros, keys], axis=0)
    values_pad = jnp.concatenate([zeros, values], axis=0)
    sink_group = (jnp.arange(G * SINKS, dtype=jnp.int32) // SINKS).astype(jnp.int32)
    slot = jnp.arange(G * W, dtype=jnp.int32)

    def one_block(number):
        first = (number * block).astype(jnp.int32)
        index = first + jnp.arange(block, dtype=jnp.int32)
        req_q, off_q, grp_q = describe(index, starts, suffix_lengths, request_group)
        near = first - W + jnp.arange(W + block, dtype=jnp.int32)
        req_k, off_k, grp_k = describe(near, starts, suffix_lengths, request_group)
        mask_sink = grp_q[:, None] == sink_group[None, :]
        mask_cache = (grp_q[:, None] == (slot // W)[None, :]) & ((slot % W)[None, :] > off_q[:, None])
        mask_suf = (req_k[None, :] == req_q[:, None]) & (near[None, :] <= index[:, None]) & (index[:, None] - near[None, :] < W) & (near[None, :] >= 0)
        mask = jnp.concatenate([mask_sink, mask_cache, mask_suf], axis=1)
        near_k = lax.dynamic_slice_in_dim(keys_pad, first, W + block, 0)
        near_v = lax.dynamic_slice_in_dim(values_pad, first, W + block, 0)
        all_k = jnp.concatenate([sink_k, cache_k, near_k], axis=0).astype(jnp.float32).reshape(-1, HEADS, HD)
        all_v = jnp.concatenate([sink_v, cache_v, near_v], axis=0).astype(jnp.float32).reshape(-1, HEADS, HD)
        q_block = lax.dynamic_slice_in_dim(queries, first, block, 0).astype(jnp.float32).reshape(block, HEADS, HD)
        score = jnp.einsum('qhd,khd->hqk', q_block, all_k) * scale
        score = jnp.where(mask[None], score, jnp.float32(-1e+30))
        top = lax.optimization_barrier(jnp.max(score, axis=2, keepdims=True))
        prob = jnp.where(mask[None], jnp.exp(score - top), jnp.float32(0.0))
        den = lax.optimization_barrier(jnp.sum(prob, axis=2))
        weights = lax.optimization_barrier(prob.astype(jnp.bfloat16)).astype(jnp.float32)
        num = jnp.einsum('hqk,khd->hqd', weights, all_v)
        attn = (num / den[:, :, None]).transpose(1, 0, 2).reshape(block, HC)
        return attn.astype(jnp.bfloat16)
    attn = lax.map(one_block, jnp.arange(SUF // block, dtype=jnp.int32)).reshape(SUF, HC)
    out = jnp.dot(attn.astype(jnp.float32), w_out.astype(jnp.float32), preferred_element_type=jnp.float32)
    return out.T.astype(jnp.bfloat16)
```

```python
import functools
import math

import jax
import jax.numpy as jnp
from jax import lax
from jax.experimental import pallas as pl
from jax.experimental.pallas import tpu as pltpu
from jax.sharding import PartitionSpec as P

HD = 96
W = 1024
SINKS = 4


def starts_of(lengths):
    place = jnp.arange(lengths.shape[0], dtype=jnp.int32)
    return jnp.sum(jnp.where(place[None, :] < place[:, None], lengths[None, :], 0), axis=1)


def from_behind(array, axis, by):
    devices = lax.axis_size(axis)
    pairs = [(i, i + by) for i in range(devices) if 0 <= i + by < devices]
    return lax.ppermute(array, axis, pairs)


def describe(index, starts, lengths, groups):
    inside = (starts[None, :] <= index[:, None]) & (index[:, None] < (starts + lengths)[None, :])
    flag = inside.astype(jnp.int32)
    found = jnp.sum(flag, axis=1)
    request = jnp.sum(flag * jnp.arange(starts.shape[0], dtype=jnp.int32)[None, :], axis=1)
    request = jnp.where(found > 0, request, -1)
    offset = index - jnp.sum(flag * starts[None, :], axis=1)
    group = jnp.sum(flag * groups[None, :], axis=1)
    return (request, offset, group)


def gathered(
    queries, keys, values, cache_k, cache_v, sink_k, sink_v, suffix_lengths, request_group, w_out
):
    rows, width = queries.shape
    heads = width // HD
    scale = 1.0 / math.sqrt(HD)
    device = lax.axis_index("seq")
    starts = starts_of(suffix_lengths)
    index = device * rows + jnp.arange(rows, dtype=jnp.int32)
    req_q, off_q, grp_q = describe(index, starts, suffix_lengths, request_group)
    q_three = queries.reshape(rows, heads, HD)

    def absorb(state, key_rows, value_rows, mask):
        top, den, acc = state
        count = key_rows.shape[0]
        k_three = key_rows.reshape(count, heads, HD)
        v_three = value_rows.reshape(count, heads, HD)
        score = (
            jnp.einsum("shd,khd->hsk", q_three, k_three, preferred_element_type=jnp.float32) * scale
        )
        score = jnp.where(mask[None], score, jnp.float32(-1e30))
        new_top = jnp.maximum(top, jnp.max(score, axis=2))
        factor = jnp.exp(top - new_top)
        prob = jnp.where(mask[None], jnp.exp(score - new_top[:, :, None]), jnp.float32(0.0))
        den = den * factor + jnp.sum(prob, axis=2)
        part = jnp.einsum(
            "hsk,khd->hsd", prob.astype(jnp.bfloat16), v_three, preferred_element_type=jnp.float32
        )
        acc = acc * factor[:, :, None] + part
        return (new_top, den, acc)

    def suffix_mask(near):
        req_k, off_k, grp_k = describe(near, starts, suffix_lengths, request_group)
        return (
            (req_k[None, :] == req_q[:, None])
            & (near[None, :] <= index[:, None])
            & (index[:, None] - near[None, :] < W)
            & (near[None, :] >= 0)
        )

    state = (
        jnp.full((heads, rows), -1e30, jnp.float32),
        jnp.zeros((heads, rows), jnp.float32),
        jnp.zeros((heads, rows, HD), jnp.float32),
    )
    sink_group = jnp.arange(sink_k.shape[0], dtype=jnp.int32) // SINKS
    state = absorb(state, sink_k, sink_v, grp_q[:, None] == sink_group[None, :])
    pieces = (
        lax.all_gather(cache_k, "seq", axis=0, tiled=True),
        lax.all_gather(cache_v, "seq", axis=0, tiled=True),
    )
    slot = jnp.arange(pieces[0].shape[0], dtype=jnp.int32)
    state = absorb(
        state,
        pieces[0],
        pieces[1],
        (grp_q[:, None] == (slot // W)[None, :]) & ((slot % W)[None, :] > off_q[:, None]),
    )
    state = absorb(state, keys, values, suffix_mask(index))
    reach = W // rows
    current = (keys, values)
    for step in range(1, reach + 1):
        current = from_behind((current[0], current[1]), "seq", 1)
        near = (device - step) * rows + jnp.arange(rows, dtype=jnp.int32)
        state = absorb(state, current[0], current[1], suffix_mask(near))
    top, den, acc = state
    attn = (acc / den[:, :, None]).transpose(1, 0, 2).reshape(rows, width).astype(jnp.bfloat16)
    return lax.psum_scatter(
        jnp.einsum("cd,sc->ds", w_out, attn, preferred_element_type=jnp.float32).astype(
            jnp.bfloat16
        ),
        "head",
        scatter_dimension=0,
        tiled=True,
    )


TILE = 256


def greet(me, n):
    barrier = pltpu.get_barrier_semaphore()

    def one(o, carry):
        pl.semaphore_signal(
            barrier,
            inc=1,
            device_id={"seq": lax.rem(me + o, n)},
            device_id_type=pl.DeviceIdType.MESH,
        )
        return carry

    lax.fori_loop(1, n, one, 0)
    pl.semaphore_wait(barrier, n - 1)


def exchange(me, n, source, landing, send_sem, recv_sem, local_sem):
    def copy_to(o):
        to = lax.rem(me + o, n)
        return pltpu.make_async_remote_copy(
            src_ref=source.at[to],
            dst_ref=landing.at[me],
            send_sem=send_sem.at[o],
            recv_sem=recv_sem.at[o],
            device_id={"seq": to},
            device_id_type=pl.DeviceIdType.MESH,
        )

    def start(o, carry):
        copy_to(o).start()
        return carry

    def finish(o, carry):
        copy_to(o).wait()
        return carry

    own = pltpu.make_async_copy(source.at[me], landing.at[me], local_sem)
    lax.fori_loop(1, n, start, 0)
    own.start()
    lax.fori_loop(1, n, finish, 0)
    own.wait()


def to_heads_kernel(n, q, k, v, ck, cv, out, stage, send_sem, recv_sem, local_sem):
    me = lax.axis_index("seq")
    rows = q.shape[0]
    for a, ref in enumerate((q, k, v, ck, cv)):
        for g in range(n // 4):
            turned = ref[:, g * 4 * HD : (g + 1) * 4 * HD].T
            for i in range(4):
                stage[4 * g + i, a] = turned[i * HD : (i + 1) * HD]
    greet(me, n)
    exchange(me, n, stage, out, send_sem, recv_sem, local_sem)


def to_heads(n, *arrays):
    rows = arrays[0].shape[0]
    shape = (n, len(arrays), HD, rows)
    return pl.pallas_call(
        functools.partial(to_heads_kernel, n),
        out_shape=jax.ShapeDtypeStruct(shape, jnp.bfloat16),
        in_specs=[pl.BlockSpec(memory_space=pltpu.VMEM)] * len(arrays),
        out_specs=pl.BlockSpec(memory_space=pl.ANY),
        scratch_shapes=[
            pltpu.VMEM(shape, jnp.bfloat16),
            pltpu.SemaphoreType.DMA((n,)),
            pltpu.SemaphoreType.DMA((n,)),
            pltpu.SemaphoreType.DMA,
        ],
        compiler_params=pltpu.CompilerParams(
            collective_id=0, has_side_effects=True, vmem_limit_bytes=32 << 20
        ),
        name="to_heads",
    )(*arrays)


def attend_kernel(
    tokens, slots, lengths, groups, info, x, sk, sv, out, q_t, v_t, cv_t, k_n, ck_n
):
    n, _, _, rows = x.shape
    count = lengths.shape[0]
    own = slots // W
    factor = math.log2(math.e) / math.sqrt(HD)
    for b in range(n):
        at = pl.ds(b * rows, rows)
        q_t[:, at] = x[b, 0]
        k_n[at, :] = x[b, 1].T
        v_t[:, at] = x[b, 2]
        ck_n[at, :] = x[b, 3].T
        cv_t[:, at] = x[b, 4]
    column = lax.broadcasted_iota(jnp.int32, (TILE, 1), 0)
    sink_column = lax.broadcasted_iota(jnp.int32, (sk.shape[0], 1), 0) // SINKS

    def tile(i, carry):
        first = i * TILE
        last = first + TILE
        begin = jnp.int32(0)
        earliest = first
        lowest = [jnp.int32(W) for _ in range(own)]
        for r in range(count):
            end = begin + lengths[r]
            low = jnp.maximum(first, begin)
            touches = low < jnp.minimum(last, end)
            earliest = jnp.where(touches, jnp.minimum(earliest, begin), earliest)
            for g in range(own):
                lowest[g] = jnp.where(
                    touches & (groups[r] == g), jnp.minimum(lowest[g], low - begin), lowest[g]
                )
            begin = end
        here = pl.ds(pl.multiple_of(first, TILE), TILE)
        q_tile = q_t[:, here]
        start_q = info[0:1, here]
        group_q = info[1:2, here]
        index_q = first + lax.broadcasted_iota(jnp.int32, (1, TILE), 1)
        offset_q = index_q - start_q

        score = jnp.dot(sk[...], q_tile, preferred_element_type=jnp.float32)
        score = jnp.where(sink_column == group_q, score, jnp.float32(-1e30))
        top = jnp.max(score, axis=0, keepdims=True)
        prob = jnp.exp2((score - top) * factor)
        den = jnp.sum(prob, axis=0, keepdims=True)
        acc = jnp.dot(sv[...], prob.astype(jnp.bfloat16), preferred_element_type=jnp.float32)

        def absorb(state, key_rows, value_columns, mask):
            top, den, acc = state
            score = jnp.dot(key_rows, q_tile, preferred_element_type=jnp.float32)
            score = jnp.where(mask, score, jnp.float32(-1e30))
            new_top = jnp.maximum(top, jnp.max(score, axis=0, keepdims=True))
            shrink = jnp.exp2((top - new_top) * factor)
            prob = jnp.exp2((score - new_top) * factor)
            den = den * shrink + jnp.sum(prob, axis=0, keepdims=True)
            acc = acc * shrink + jnp.dot(
                value_columns, prob.astype(jnp.bfloat16), preferred_element_type=jnp.float32
            )
            return new_top, den, acc

        state = (top, den, acc)
        for g in range(own):
            limit = jnp.where(group_q == g, offset_q, jnp.int32(W))

            def cached(c, state):
                at = pl.ds(pl.multiple_of(g * W + c * TILE, TILE), TILE)
                mask = c * TILE + column > limit
                return absorb(state, ck_n[at, :], cv_t[:, at], mask)

            state = lax.fori_loop((lowest[g] + 1) // TILE, W // TILE, cached, state)

        def suffix(c, state):
            at = pl.ds(pl.multiple_of(c * TILE, TILE), TILE)
            index_k = c * TILE + column
            return absorb(
                state, k_n[at, :], v_t[:, at], (index_k >= start_q) & (index_k <= index_q)
            )

        top, den, acc = lax.fori_loop(earliest // TILE, i + 1, suffix, state)
        result = (acc / den).astype(jnp.bfloat16)
        for part in range(TILE // rows):
            out[i * (TILE // rows) + part] = result[:, part * rows : (part + 1) * rows]
        return carry

    lax.fori_loop(0, tokens // TILE, tile, 0)


def attend(x, sk, sv, lengths, groups, info):
    n, _, _, rows = x.shape
    tokens = n * rows
    vmem = pl.BlockSpec(memory_space=pltpu.VMEM)
    smem = pl.BlockSpec(memory_space=pltpu.SMEM)
    return pl.pallas_call(
        functools.partial(attend_kernel, tokens, tokens),
        out_shape=jax.ShapeDtypeStruct((n, HD, rows), jnp.bfloat16),
        in_specs=[smem, smem, vmem, vmem, vmem, vmem],
        out_specs=vmem,
        scratch_shapes=[
            pltpu.VMEM((HD, tokens), jnp.bfloat16),
            pltpu.VMEM((HD, tokens), jnp.bfloat16),
            pltpu.VMEM((HD, tokens), jnp.bfloat16),
            pltpu.VMEM((tokens, HD), jnp.bfloat16),
            pltpu.VMEM((tokens, HD), jnp.bfloat16),
        ],
        compiler_params=pltpu.CompilerParams(vmem_limit_bytes=32 << 20),
        name="attend",
    )(lengths, groups, info, x, sk, sv)


def to_tokens_kernel(n, x, out, send_sem, recv_sem, local_sem):
    me = lax.axis_index("seq")
    greet(me, n)
    exchange(me, n, x, out, send_sem, recv_sem, local_sem)


def to_tokens(x):
    n = x.shape[0]
    return pl.pallas_call(
        functools.partial(to_tokens_kernel, n),
        out_shape=jax.ShapeDtypeStruct(x.shape, x.dtype),
        in_specs=[pl.BlockSpec(memory_space=pltpu.VMEM)],
        out_specs=pl.BlockSpec(memory_space=pl.ANY),
        scratch_shapes=[
            pltpu.SemaphoreType.DMA((n,)),
            pltpu.SemaphoreType.DMA((n,)),
            pltpu.SemaphoreType.DMA,
        ],
        compiler_params=pltpu.CompilerParams(collective_id=1, has_side_effects=True),
        name="to_tokens",
    )(x)


def by_heads(
    queries, keys, values, cache_k, cache_v, sink_k, sink_v, suffix_lengths, request_group, w_out
):
    n = lax.axis_size("seq")
    rows, width = queries.shape
    starts = starts_of(suffix_lengths)
    index = jnp.arange(n * rows, dtype=jnp.int32)
    inside = (starts[:, None] <= index[None, :]) & (
        index[None, :] < (starts + suffix_lengths)[:, None]
    )
    info = jnp.stack(
        [
            jnp.sum(jnp.where(inside, starts[:, None], 0), axis=0),
            jnp.sum(jnp.where(inside, request_group[:, None], 0), axis=0),
        ]
    )
    me = lax.axis_index("seq")
    sk = lax.dynamic_slice_in_dim(sink_k, me * HD, HD, 1)
    sv = lax.dynamic_slice_in_dim(sink_v, me * HD, HD, 1).T
    x = to_heads(n, queries, keys, values, cache_k, cache_v)
    attn = attend(x, sk, sv, suffix_lengths, request_group, info)
    attn = to_tokens(attn).reshape(width, rows)
    return lax.psum_scatter(
        jnp.einsum("cd,cs->ds", w_out, attn, preferred_element_type=jnp.float32).astype(
            jnp.bfloat16
        ),
        "head",
        scatter_dimension=0,
        tiled=True,
    )


def shards(queries, keys, values, cache_k, *rest):
    n = lax.axis_size("seq")
    rows, width = queries.shape
    fits = (
        n == width // HD
        and n % 4 == 0
        and rows % 128 == 0
        and TILE % rows == 0
        and cache_k.shape[0] == rows
        and (n * rows) % W == 0
    )
    return (by_heads if fits else gathered)(queries, keys, values, cache_k, *rest)


def solution(mesh):
    placed = (
        P("seq", "head"),
        P("seq", "head"),
        P("seq", "head"),
        P("seq", "head"),
        P("seq", "head"),
        P(None, "head"),
        P(None, "head"),
        P(),
        P(),
        P("head", None),
    )
    return jax.shard_map(
        shards, mesh=mesh, in_specs=placed, out_specs=P("head", "seq"), check_vma=False
    )
```

```python
import functools
import math

import jax
import jax.numpy as jnp
from jax import lax
from jax.experimental import pallas as pl
from jax.experimental.pallas import tpu as pltpu
from jax.sharding import PartitionSpec as P

HD = 96
W = 1024
SINKS = 4


def starts_of(lengths):
    place = jnp.arange(lengths.shape[0], dtype=jnp.int32)
    return jnp.sum(jnp.where(place[None, :] < place[:, None], lengths[None, :], 0), axis=1)


def from_behind(array, axis, by):
    devices = lax.axis_size(axis)
    pairs = [(i, i + by) for i in range(devices) if 0 <= i + by < devices]
    return lax.ppermute(array, axis, pairs)


def describe(index, starts, lengths, groups):
    inside = (starts[None, :] <= index[:, None]) & (index[:, None] < (starts + lengths)[None, :])
    flag = inside.astype(jnp.int32)
    found = jnp.sum(flag, axis=1)
    request = jnp.sum(flag * jnp.arange(starts.shape[0], dtype=jnp.int32)[None, :], axis=1)
    request = jnp.where(found > 0, request, -1)
    offset = index - jnp.sum(flag * starts[None, :], axis=1)
    group = jnp.sum(flag * groups[None, :], axis=1)
    return (request, offset, group)


def gathered(
    queries, keys, values, cache_k, cache_v, sink_k, sink_v, suffix_lengths, request_group, w_out
):
    rows, width = queries.shape
    heads = width // HD
    scale = 1.0 / math.sqrt(HD)
    device = lax.axis_index("seq")
    starts = starts_of(suffix_lengths)
    index = device * rows + jnp.arange(rows, dtype=jnp.int32)
    req_q, off_q, grp_q = describe(index, starts, suffix_lengths, request_group)
    q_three = queries.reshape(rows, heads, HD)

    def absorb(state, key_rows, value_rows, mask):
        top, den, acc = state
        count = key_rows.shape[0]
        k_three = key_rows.reshape(count, heads, HD)
        v_three = value_rows.reshape(count, heads, HD)
        score = (
            jnp.einsum("shd,khd->hsk", q_three, k_three, preferred_element_type=jnp.float32) * scale
        )
        score = jnp.where(mask[None], score, jnp.float32(-1e30))
        new_top = jnp.maximum(top, jnp.max(score, axis=2))
        factor = jnp.exp(top - new_top)
        prob = jnp.where(mask[None], jnp.exp(score - new_top[:, :, None]), jnp.float32(0.0))
        den = den * factor + jnp.sum(prob, axis=2)
        part = jnp.einsum(
            "hsk,khd->hsd", prob.astype(jnp.bfloat16), v_three, preferred_element_type=jnp.float32
        )
        acc = acc * factor[:, :, None] + part
        return (new_top, den, acc)

    def suffix_mask(near):
        req_k, off_k, grp_k = describe(near, starts, suffix_lengths, request_group)
        return (
            (req_k[None, :] == req_q[:, None])
            & (near[None, :] <= index[:, None])
            & (index[:, None] - near[None, :] < W)
            & (near[None, :] >= 0)
        )

    state = (
        jnp.full((heads, rows), -1e30, jnp.float32),
        jnp.zeros((heads, rows), jnp.float32),
        jnp.zeros((heads, rows, HD), jnp.float32),
    )
    sink_group = jnp.arange(sink_k.shape[0], dtype=jnp.int32) // SINKS
    state = absorb(state, sink_k, sink_v, grp_q[:, None] == sink_group[None, :])
    pieces = (
        lax.all_gather(cache_k, "seq", axis=0, tiled=True),
        lax.all_gather(cache_v, "seq", axis=0, tiled=True),
    )
    slot = jnp.arange(pieces[0].shape[0], dtype=jnp.int32)
    state = absorb(
        state,
        pieces[0],
        pieces[1],
        (grp_q[:, None] == (slot // W)[None, :]) & ((slot % W)[None, :] > off_q[:, None]),
    )
    state = absorb(state, keys, values, suffix_mask(index))
    reach = W // rows
    current = (keys, values)
    for step in range(1, reach + 1):
        current = from_behind((current[0], current[1]), "seq", 1)
        near = (device - step) * rows + jnp.arange(rows, dtype=jnp.int32)
        state = absorb(state, current[0], current[1], suffix_mask(near))
    top, den, acc = state
    attn = (acc / den[:, :, None]).transpose(1, 0, 2).reshape(rows, width).astype(jnp.bfloat16)
    return lax.psum_scatter(
        jnp.einsum("cd,sc->ds", w_out, attn, preferred_element_type=jnp.float32).astype(
            jnp.bfloat16
        ),
        "head",
        scatter_dimension=0,
        tiled=True,
    )


TILE = 256


def greet(me, n, extra=()):
    barrier = pltpu.get_barrier_semaphore()

    def one(o, carry):
        pl.semaphore_signal(
            barrier,
            inc=1,
            device_id={"seq": lax.rem(me + o, n)},
            device_id_type=pl.DeviceIdType.MESH,
        )
        return carry

    lax.fori_loop(1, n, one, 0)
    for other in extra:
        pl.semaphore_signal(
            barrier, inc=1, device_id={"head": other}, device_id_type=pl.DeviceIdType.MESH
        )


def greeted(count):
    pl.semaphore_wait(pltpu.get_barrier_semaphore(), count)


def exchange(me, n, source, landing, send_sem, recv_sem, local_sem):
    def copy_to(o):
        to = lax.rem(me + o, n)
        return pltpu.make_async_remote_copy(
            src_ref=source.at[to],
            dst_ref=landing.at[me],
            send_sem=send_sem.at[o],
            recv_sem=recv_sem.at[o],
            device_id={"seq": to},
            device_id_type=pl.DeviceIdType.MESH,
        )

    def one_start(o, carry):
        copy_to(o).start()
        return carry

    def one_end(o, carry):
        copy_to(o).wait()
        return carry

    own = pltpu.make_async_copy(source.at[me], landing.at[me], local_sem)

    def start():
        lax.fori_loop(1, n, one_start, 0)
        own.start()

    def end():
        lax.fori_loop(1, n, one_end, 0)
        own.wait()

    return start, end


def to_heads_kernel(n, *refs):
    five, (first, second), refs = refs[:5], refs[5:7], refs[7:]
    raw, stage_one, stage_two, load_sem, send_sem, recv_sem, local_sem = refs
    me = lax.axis_index("seq")
    loads = [pltpu.make_async_copy(five[a], raw.at[a], load_sem.at[a]) for a in range(5)]
    for load in loads:
        load.start()
    greet(me, n)
    ends = []
    for which, (stage, landing, arrays) in enumerate(
        ((stage_one, first, (0, 1, 2)), (stage_two, second, (3, 4)))
    ):
        for place, a in enumerate(arrays):
            loads[a].wait()
            for g in range(n // 4):
                turned = raw[a, :, g * 4 * HD : (g + 1) * 4 * HD].T
                for i in range(4):
                    stage[4 * g + i, place] = turned[i * HD : (i + 1) * HD]
        if which == 0:
            greeted(n - 1)
        start, end = exchange(
            me, n, stage, landing, send_sem.at[which], recv_sem.at[which], local_sem.at[which]
        )
        start()
        ends.append(end)
    for end in ends:
        end()


def to_heads(n, *arrays):
    rows, width = arrays[0].shape
    shapes = [(n, 3, HD, rows), (n, 2, HD, rows)]
    anywhere = pl.BlockSpec(memory_space=pl.ANY)
    return pl.pallas_call(
        functools.partial(to_heads_kernel, n),
        out_shape=[jax.ShapeDtypeStruct(shape, jnp.bfloat16) for shape in shapes],
        in_specs=[anywhere] * 5,
        out_specs=[anywhere] * 2,
        scratch_shapes=[
            pltpu.VMEM((5, rows, width), jnp.bfloat16),
            pltpu.VMEM(shapes[0], jnp.bfloat16),
            pltpu.VMEM(shapes[1], jnp.bfloat16),
            pltpu.SemaphoreType.DMA((5,)),
            pltpu.SemaphoreType.DMA((2, n)),
            pltpu.SemaphoreType.DMA((2, n)),
            pltpu.SemaphoreType.DMA((2,)),
        ],
        compiler_params=pltpu.CompilerParams(
            collective_id=0, has_side_effects=True, vmem_limit_bytes=48 << 20
        ),
        name="to_heads",
    )(*arrays)


def attend_kernel(tokens, slots, lengths, groups, one, two, sk, sv, out, q_t, k_n, v_t):
    n, _, _, rows = one.shape
    count = lengths.shape[0]
    own = slots // W
    factor = math.log2(math.e) / math.sqrt(HD)
    for b in range(n):
        at = pl.ds(b * rows, rows)
        later = pl.ds(slots + b * rows, rows)
        q_t[:, at] = one[b, 0]
        k_n[later, :] = one[b, 1].T
        v_t[:, later] = one[b, 2]
        k_n[at, :] = two[b, 0].T
        v_t[:, at] = two[b, 1]
    column = lax.broadcasted_iota(jnp.int32, (TILE, 1), 0)
    sink_column = lax.broadcasted_iota(jnp.int32, (sk.shape[0], 1), 0) // SINKS
    far = jnp.int32(1 << 30)

    def tile(i, carry):
        first = i * TILE
        last = first + TILE
        index_q = first + lax.broadcasted_iota(jnp.int32, (1, TILE), 1)
        begin = jnp.int32(0)
        earliest = first
        lowest = [jnp.int32(W) for _ in range(own)]
        start_q = jnp.zeros((1, TILE), jnp.int32)
        group_q = jnp.zeros((1, TILE), jnp.int32)
        for r in range(count):
            end = begin + lengths[r]
            low = jnp.maximum(first, begin)
            touches = low < jnp.minimum(last, end)
            earliest = jnp.where(touches, jnp.minimum(earliest, begin), earliest)
            for g in range(own):
                lowest[g] = jnp.where(
                    touches & (groups[r] == g), jnp.minimum(lowest[g], low - begin), lowest[g]
                )
            inside = index_q >= begin
            start_q = jnp.where(inside, begin, start_q)
            group_q = jnp.where(inside, groups[r], group_q)
            begin = end
        offset_q = index_q - start_q
        sections = []
        for g in range(own):
            chunk = (lowest[g] + 1) // TILE
            limit = g * W + jnp.where(group_q == g, offset_q, jnp.int32(W))
            sections.append(
                (g * (W // TILE) + chunk, W // TILE - chunk, limit, jnp.zeros_like(limit) + far)
            )
        chunk = earliest // TILE
        sections.append(
            (slots // TILE + chunk, i + 1 - chunk, slots + start_q - 1, slots + index_q)
        )
        total = sum(section[1] for section in sections)

        def find(t):
            chunk, low, high = sections[0][0] + t, sections[0][2], sections[0][3]
            before = sections[0][1]
            for begins, number, lower, upper in sections[1:]:
                here = t >= before
                chunk = jnp.where(here, begins + t - before, chunk)
                low = jnp.where(here, lower, low)
                high = jnp.where(here, upper, high)
                before = before + number
            return pl.multiple_of(chunk * TILE, TILE), low, high

        q_tile = q_t[:, pl.ds(pl.multiple_of(first, TILE), TILE)]

        def scores(t):
            at, _, _ = find(t)
            return jnp.dot(k_n[pl.ds(at, TILE), :], q_tile, preferred_element_type=jnp.float32)

        def weigh(t, prob):
            at, _, _ = find(t)
            return jnp.dot(v_t[:, pl.ds(at, TILE)], prob, preferred_element_type=jnp.float32)

        score = jnp.dot(sk[...], q_tile, preferred_element_type=jnp.float32)
        score = jnp.where(sink_column == group_q, score, jnp.float32(-1e30))
        top = jnp.max(score, axis=0, keepdims=True)
        prob = jnp.exp2((score - top) * factor)
        den = jnp.sum(prob, axis=0, keepdims=True)
        acc = jnp.dot(sv[...], prob.astype(jnp.bfloat16), preferred_element_type=jnp.float32)

        def step(t, state):
            top, den, acc, score, prob = state
            following = scores(jnp.minimum(t + 1, total - 1))
            acc = acc + weigh(jnp.maximum(t - 1, 0), prob)
            at, low, high = find(t)
            index_k = at + column
            score = jnp.where((index_k > low) & (index_k <= high), score, jnp.float32(-1e30))
            new_top = jnp.maximum(top, jnp.max(score, axis=0, keepdims=True))
            shrink = jnp.exp2((top - new_top) * factor)
            prob = jnp.exp2((score - new_top) * factor)
            den = den * shrink + jnp.sum(prob, axis=0, keepdims=True)
            return new_top, den, acc * shrink, following, prob.astype(jnp.bfloat16)

        state = (top, den, acc, scores(0), jnp.zeros((TILE, TILE), jnp.bfloat16))
        top, den, acc, score, prob = lax.fori_loop(0, total, step, state)
        acc = acc + weigh(total - 1, prob)
        result = (acc / den).astype(jnp.bfloat16)
        for part in range(TILE // rows):
            out[i * (TILE // rows) + part] = result[:, part * rows : (part + 1) * rows]
        return carry

    lax.fori_loop(0, tokens // TILE, tile, 0)


def attend(one, two, sk, sv, lengths, groups):
    n, _, _, rows = one.shape
    tokens = slots = n * rows
    vmem = pl.BlockSpec(memory_space=pltpu.VMEM)
    smem = pl.BlockSpec(memory_space=pltpu.SMEM)
    return pl.pallas_call(
        functools.partial(attend_kernel, tokens, slots),
        out_shape=jax.ShapeDtypeStruct((n, HD, rows), jnp.bfloat16),
        in_specs=[smem, smem, vmem, vmem, vmem, vmem],
        out_specs=vmem,
        scratch_shapes=[
            pltpu.VMEM((HD, tokens), jnp.bfloat16),
            pltpu.VMEM((slots + tokens, HD), jnp.bfloat16),
            pltpu.VMEM((HD, slots + tokens), jnp.bfloat16),
        ],
        compiler_params=pltpu.CompilerParams(vmem_limit_bytes=48 << 20),
        name="attend",
    )(lengths, groups, one, two, sk, sv)


def project_kernel(n, x, w, out, *scratch):
    landed, w_v, turned, sent, came = scratch[:5]
    send_sem, recv_sem, local_sem, w_sem, over_sem, back_sem = scratch[5:]
    me = lax.axis_index("seq")
    mine = lax.axis_index("head")
    other = 1 - mine
    width, features = w.shape
    half = features // 2
    parts, piece, rows = sent.shape
    loads = []
    for number, side in enumerate((other, mine)):
        at = pl.ds(pl.multiple_of(side * half, half), half)
        loads.append(pltpu.make_async_copy(w.at[:, at], w_v.at[number], w_sem.at[number]))
    greet(me, n, (other,))
    for load in loads:
        load.start()
    greeted(n)
    start, end = exchange(me, n, x, landed, send_sem, recv_sem, local_sem)
    start()
    end()
    turned[...] = landed[...].reshape(width, rows).T

    def share(number, j):
        at = pl.ds(pl.multiple_of(j * piece, piece), piece)
        return jnp.dot(
            turned[...], w_v[number, :, at], preferred_element_type=jnp.float32
        ).T

    def over(j):
        return pltpu.make_async_remote_copy(
            src_ref=sent.at[j],
            dst_ref=came.at[j],
            send_sem=over_sem.at[j],
            recv_sem=back_sem.at[j],
            device_id={"head": other},
            device_id_type=pl.DeviceIdType.MESH,
        )

    def theirs(j, carry):
        sent[j] = share(0, j).astype(jnp.bfloat16)
        over(j).start()
        return carry

    def ours(j, carry):
        part = share(1, j)
        over(j).wait()
        at = pl.ds(pl.multiple_of(j * piece, piece), piece)
        out[at, :] = (part + came[j].astype(jnp.float32)).astype(jnp.bfloat16)
        return carry

    loads[0].wait()
    lax.fori_loop(0, parts, theirs, 0)
    loads[1].wait()
    lax.fori_loop(0, parts, ours, 0)


def project(x, w):
    n, _, rows = x.shape
    width, features = w.shape
    half = features // 2
    parts = half // TILE
    return pl.pallas_call(
        functools.partial(project_kernel, n),
        out_shape=jax.ShapeDtypeStruct((half, rows), x.dtype),
        in_specs=[pl.BlockSpec(memory_space=pltpu.VMEM), pl.BlockSpec(memory_space=pl.ANY)],
        out_specs=pl.BlockSpec(memory_space=pltpu.VMEM),
        scratch_shapes=[
            pltpu.VMEM(x.shape, jnp.bfloat16),
            pltpu.VMEM((2, width, half), jnp.bfloat16),
            pltpu.VMEM((rows, width), jnp.bfloat16),
            pltpu.VMEM((parts, TILE, rows), jnp.bfloat16),
            pltpu.VMEM((parts, TILE, rows), jnp.bfloat16),
            pltpu.SemaphoreType.DMA((n,)),
            pltpu.SemaphoreType.DMA((n,)),
            pltpu.SemaphoreType.DMA,
            pltpu.SemaphoreType.DMA((2,)),
            pltpu.SemaphoreType.DMA((parts,)),
            pltpu.SemaphoreType.DMA((parts,)),
        ],
        compiler_params=pltpu.CompilerParams(
            collective_id=1, has_side_effects=True, vmem_limit_bytes=48 << 20
        ),
        name="project",
    )(x, w)


def by_heads(
    queries, keys, values, cache_k, cache_v, sink_k, sink_v, suffix_lengths, request_group, w_out
):
    n = lax.axis_size("seq")
    me = lax.axis_index("seq")
    sk = lax.dynamic_slice_in_dim(sink_k, me * HD, HD, 1)
    sv = lax.dynamic_slice_in_dim(sink_v, me * HD, HD, 1).T
    one, two = to_heads(n, queries, keys, values, cache_k, cache_v)
    attn = attend(one, two, sk, sv, suffix_lengths, request_group)
    return project(attn, w_out)


def shards(queries, keys, values, cache_k, *rest):
    n = lax.axis_size("seq")
    rows, width = queries.shape
    fits = (
        n == width // HD
        and n % 4 == 0
        and rows % 128 == 0
        and TILE % rows == 0
        and cache_k.shape[0] == rows
        and (n * rows) % W == 0
        and lax.axis_size("head") == 2
        and rest[-1].shape[1] % (2 * TILE) == 0
    )
    return (by_heads if fits else gathered)(queries, keys, values, cache_k, *rest)


def solution(mesh):
    placed = (
        P("seq", "head"),
        P("seq", "head"),
        P("seq", "head"),
        P("seq", "head"),
        P("seq", "head"),
        P(None, "head"),
        P(None, "head"),
        P(),
        P(),
        P("head", None),
    )
    return jax.shard_map(
        shards, mesh=mesh, in_specs=placed, out_specs=P("head", "seq"), check_vma=False
    )
```

```python
import functools
import math

import jax
import jax.numpy as jnp
from jax import lax
from jax.experimental import pallas as pl
from jax.experimental.pallas import tpu as pltpu
from jax.sharding import PartitionSpec as P

HD = 96
W = 1024
SINKS = 4


def starts_of(lengths):
    place = jnp.arange(lengths.shape[0], dtype=jnp.int32)
    return jnp.sum(jnp.where(place[None, :] < place[:, None], lengths[None, :], 0), axis=1)


def from_behind(array, axis, by):
    devices = lax.axis_size(axis)
    pairs = [(i, i + by) for i in range(devices) if 0 <= i + by < devices]
    return lax.ppermute(array, axis, pairs)


def describe(index, starts, lengths, groups):
    inside = (starts[None, :] <= index[:, None]) & (index[:, None] < (starts + lengths)[None, :])
    flag = inside.astype(jnp.int32)
    found = jnp.sum(flag, axis=1)
    request = jnp.sum(flag * jnp.arange(starts.shape[0], dtype=jnp.int32)[None, :], axis=1)
    request = jnp.where(found > 0, request, -1)
    offset = index - jnp.sum(flag * starts[None, :], axis=1)
    group = jnp.sum(flag * groups[None, :], axis=1)
    return (request, offset, group)


def gathered(
    queries, keys, values, cache_k, cache_v, sink_k, sink_v, suffix_lengths, request_group, w_out
):
    rows, width = queries.shape
    heads = width // HD
    scale = 1.0 / math.sqrt(HD)
    device = lax.axis_index("seq")
    starts = starts_of(suffix_lengths)
    index = device * rows + jnp.arange(rows, dtype=jnp.int32)
    req_q, off_q, grp_q = describe(index, starts, suffix_lengths, request_group)
    q_three = queries.reshape(rows, heads, HD)

    def absorb(state, key_rows, value_rows, mask):
        top, den, acc = state
        count = key_rows.shape[0]
        k_three = key_rows.reshape(count, heads, HD)
        v_three = value_rows.reshape(count, heads, HD)
        score = (
            jnp.einsum("shd,khd->hsk", q_three, k_three, preferred_element_type=jnp.float32) * scale
        )
        score = jnp.where(mask[None], score, jnp.float32(-1e30))
        new_top = jnp.maximum(top, jnp.max(score, axis=2))
        factor = jnp.exp(top - new_top)
        prob = jnp.where(mask[None], jnp.exp(score - new_top[:, :, None]), jnp.float32(0.0))
        den = den * factor + jnp.sum(prob, axis=2)
        part = jnp.einsum(
            "hsk,khd->hsd", prob.astype(jnp.bfloat16), v_three, preferred_element_type=jnp.float32
        )
        acc = acc * factor[:, :, None] + part
        return (new_top, den, acc)

    def suffix_mask(near):
        req_k, off_k, grp_k = describe(near, starts, suffix_lengths, request_group)
        return (
            (req_k[None, :] == req_q[:, None])
            & (near[None, :] <= index[:, None])
            & (index[:, None] - near[None, :] < W)
            & (near[None, :] >= 0)
        )

    state = (
        jnp.full((heads, rows), -1e30, jnp.float32),
        jnp.zeros((heads, rows), jnp.float32),
        jnp.zeros((heads, rows, HD), jnp.float32),
    )
    sink_group = jnp.arange(sink_k.shape[0], dtype=jnp.int32) // SINKS
    state = absorb(state, sink_k, sink_v, grp_q[:, None] == sink_group[None, :])
    pieces = (
        lax.all_gather(cache_k, "seq", axis=0, tiled=True),
        lax.all_gather(cache_v, "seq", axis=0, tiled=True),
    )
    slot = jnp.arange(pieces[0].shape[0], dtype=jnp.int32)
    state = absorb(
        state,
        pieces[0],
        pieces[1],
        (grp_q[:, None] == (slot // W)[None, :]) & ((slot % W)[None, :] > off_q[:, None]),
    )
    state = absorb(state, keys, values, suffix_mask(index))
    reach = W // rows
    current = (keys, values)
    for step in range(1, reach + 1):
        current = from_behind((current[0], current[1]), "seq", 1)
        near = (device - step) * rows + jnp.arange(rows, dtype=jnp.int32)
        state = absorb(state, current[0], current[1], suffix_mask(near))
    top, den, acc = state
    attn = (acc / den[:, :, None]).transpose(1, 0, 2).reshape(rows, width).astype(jnp.bfloat16)
    return lax.psum_scatter(
        jnp.einsum("cd,sc->ds", w_out, attn, preferred_element_type=jnp.float32).astype(
            jnp.bfloat16
        ),
        "head",
        scatter_dimension=0,
        tiled=True,
    )


TILE = 256


def greet(me, n, extra=()):
    barrier = pltpu.get_barrier_semaphore()

    def one(o, carry):
        pl.semaphore_signal(
            barrier,
            inc=1,
            device_id={"seq": lax.rem(me + o, n)},
            device_id_type=pl.DeviceIdType.MESH,
        )
        return carry

    lax.fori_loop(1, n, one, 0)
    for other in extra:
        pl.semaphore_signal(
            barrier, inc=1, device_id={"head": other}, device_id_type=pl.DeviceIdType.MESH
        )


def greeted(count):
    pl.semaphore_wait(pltpu.get_barrier_semaphore(), count)


def exchange(me, n, source, landing, send_sem, recv_sem, local_sem):
    def copy_to(o):
        to = lax.rem(me + o, n)
        return pltpu.make_async_remote_copy(
            src_ref=source.at[to],
            dst_ref=landing.at[me],
            send_sem=send_sem.at[o],
            recv_sem=recv_sem.at[o],
            device_id={"seq": to},
            device_id_type=pl.DeviceIdType.MESH,
        )

    def one_start(o, carry):
        copy_to(o).start()
        return carry

    def one_end(o, carry):
        copy_to(o).wait()
        return carry

    own = pltpu.make_async_copy(source.at[me], landing.at[me], local_sem)

    def start():
        lax.fori_loop(1, n, one_start, 0)
        own.start()

    def end():
        lax.fori_loop(1, n, one_end, 0)
        own.wait()

    return start, end


def pipelined(total, q_tile, key_rows, value_columns, limits, state):
    factor = math.log2(math.e) / math.sqrt(HD)
    column = lax.broadcasted_iota(jnp.int32, (TILE, 1), 0)

    def scores(t):
        return jnp.dot(key_rows(t), q_tile, preferred_element_type=jnp.float32)

    def weigh(t, prob):
        return jnp.dot(value_columns(t), prob, preferred_element_type=jnp.float32)

    def step(t, state):
        top, den, acc, score, prob = state
        following = scores(jnp.minimum(t + 1, total - 1))
        acc = acc + weigh(jnp.maximum(t - 1, 0), prob)
        at, low, high = limits(t)
        index_k = at + column
        seen = index_k > low
        if high is not None:
            seen = seen & (index_k <= high)
        score = jnp.where(seen, score, jnp.float32(-1e30))
        new_top = jnp.maximum(top, jnp.max(score, axis=0, keepdims=True))
        shrink = jnp.exp2((top - new_top) * factor)
        prob = jnp.exp2((score - new_top) * factor)
        den = den * shrink + jnp.sum(prob, axis=0, keepdims=True)
        return new_top, den, acc * shrink, following, prob.astype(jnp.bfloat16)

    state = (*state, scores(0), jnp.zeros((TILE, TILE), jnp.bfloat16))
    top, den, acc, _, prob = lax.fori_loop(0, total, step, state)
    return top, den, acc + weigh(total - 1, prob)


def facts(first, lengths, groups):
    index_q = first + lax.broadcasted_iota(jnp.int32, (1, TILE), 1)
    begin = jnp.int32(0)
    start_q = jnp.zeros((1, TILE), jnp.int32)
    group_q = jnp.zeros((1, TILE), jnp.int32)
    for r in range(lengths.shape[0]):
        inside = index_q >= begin
        start_q = jnp.where(inside, begin, start_q)
        group_q = jnp.where(inside, groups[r], group_q)
        begin = begin + lengths[r]
    return index_q, start_q, group_q


def to_heads_kernel(n, lengths, groups, sk, sv, *refs):
    five, (second, q_t, tops, dens, accs), refs = refs[:5], refs[5:10], refs[10:]
    raw, stage_one, stage_two, first, k_n, v_t, load_sem, send_sem, recv_sem, local_sem = refs
    me = lax.axis_index("seq")
    rows = five[0].shape[0]
    tokens = n * rows
    loads = [pltpu.make_async_copy(five[a], raw.at[a], load_sem.at[a]) for a in range(5)]
    for load in loads:
        load.start()
    greet(me, n)
    ends = []
    for which, (stage, landing, arrays) in enumerate(
        ((stage_one, first, (0, 1, 2)), (stage_two, second, (3, 4)))
    ):
        for place, a in enumerate(arrays):
            loads[a].wait()
            for g in range(n // 4):
                turned = raw[a, :, g * 4 * HD : (g + 1) * 4 * HD].T
                for i in range(4):
                    stage[4 * g + i, place] = turned[i * HD : (i + 1) * HD]
        if which == 0:
            greeted(n - 1)
        start, end = exchange(
            me, n, stage, landing, send_sem.at[which], recv_sem.at[which], local_sem.at[which]
        )
        start()
        ends.append(end)

    ends[0]()
    for b in range(n):
        at = pl.ds(b * rows, rows)
        q_t[:, at] = first[b, 0]
        k_n[at, :] = first[b, 1].T
        v_t[:, at] = first[b, 2]
    factor = math.log2(math.e) / math.sqrt(HD)
    sink_column = lax.broadcasted_iota(jnp.int32, (sk.shape[0], 1), 0) // SINKS

    def tile(i, carry):
        here = pl.ds(pl.multiple_of(i * TILE, TILE), TILE)
        index_q, start_q, group_q = facts(i * TILE, lengths, groups)
        q_tile = q_t[:, here]
        score = jnp.dot(sk[...], q_tile, preferred_element_type=jnp.float32)
        score = jnp.where(sink_column == group_q, score, jnp.float32(-1e30))
        top = jnp.max(score, axis=0, keepdims=True)
        prob = jnp.exp2((score - top) * factor)
        den = jnp.sum(prob, axis=0, keepdims=True)
        acc = jnp.dot(sv[...], prob.astype(jnp.bfloat16), preferred_element_type=jnp.float32)
        begin = jnp.maximum(i - W // TILE, 0)

        def chunk(t):
            return pl.multiple_of((begin + t) * TILE, TILE)

        top, den, acc = pipelined(
            i + 1 - begin,
            q_tile,
            lambda t: k_n[pl.ds(chunk(t), TILE), :],
            lambda t: v_t[:, pl.ds(chunk(t), TILE)],
            lambda t: (chunk(t), start_q - 1, index_q),
            (top, den, acc),
        )
        tops[:, here] = top
        dens[:, here] = den
        accs[:, here] = acc
        return carry

    lax.fori_loop(0, tokens // TILE, tile, 0)
    ends[1]()


def to_heads(n, lengths, groups, sk, sv, *arrays):
    rows, width = arrays[0].shape
    tokens = n * rows
    shapes = [(n, 3, HD, rows), (n, 2, HD, rows)]
    anywhere = pl.BlockSpec(memory_space=pl.ANY)
    vmem = pl.BlockSpec(memory_space=pltpu.VMEM)
    smem = pl.BlockSpec(memory_space=pltpu.SMEM)
    return pl.pallas_call(
        functools.partial(to_heads_kernel, n),
        out_shape=[
            jax.ShapeDtypeStruct(shapes[1], jnp.bfloat16),
            jax.ShapeDtypeStruct((HD, tokens), jnp.bfloat16),
            jax.ShapeDtypeStruct((1, tokens), jnp.float32),
            jax.ShapeDtypeStruct((1, tokens), jnp.float32),
            jax.ShapeDtypeStruct((HD, tokens), jnp.float32),
        ],
        in_specs=[smem, smem, vmem, vmem] + [anywhere] * 5,
        out_specs=[anywhere] + [vmem] * 4,
        scratch_shapes=[
            pltpu.VMEM((5, rows, width), jnp.bfloat16),
            pltpu.VMEM(shapes[0], jnp.bfloat16),
            pltpu.VMEM(shapes[1], jnp.bfloat16),
            pltpu.VMEM(shapes[0], jnp.bfloat16),
            pltpu.VMEM((tokens, HD), jnp.bfloat16),
            pltpu.VMEM((HD, tokens), jnp.bfloat16),
            pltpu.SemaphoreType.DMA((5,)),
            pltpu.SemaphoreType.DMA((2, n)),
            pltpu.SemaphoreType.DMA((2, n)),
            pltpu.SemaphoreType.DMA((2,)),
        ],
        compiler_params=pltpu.CompilerParams(
            collective_id=0, has_side_effects=True, vmem_limit_bytes=62 << 20
        ),
        name="to_heads",
    )(lengths, groups, sk, sv, *arrays)


def attend_kernel(tokens, slots, lengths, groups, two, q_t, tops, dens, accs, out, k_n, v_t):
    n, _, _, rows = two.shape
    own = slots // W
    per = W // TILE
    for b in range(n):
        at = pl.ds(b * rows, rows)
        k_n[at, :] = two[b, 0].T
        v_t[:, at] = two[b, 1]

    def tile(i, carry):
        first = i * TILE
        last = first + TILE
        index_q, start_q, group_q = facts(first, lengths, groups)
        begin = jnp.int32(0)
        lowest = [jnp.int32(W - 1) for _ in range(own)]
        for r in range(lengths.shape[0]):
            end = begin + lengths[r]
            low = jnp.maximum(first, begin)
            touches = low < jnp.minimum(last, end)
            for g in range(own):
                lowest[g] = jnp.where(
                    touches & (groups[r] == g), jnp.minimum(lowest[g], low - begin), lowest[g]
                )
            begin = end
        offset_q = index_q - start_q
        sections = []
        for g in range(own):
            chunk = (lowest[g] + 1) // TILE
            limit = g * W + jnp.where(group_q == g, offset_q, jnp.int32(W))
            sections.append((g * per + chunk, per - chunk, limit))
        total = sum(section[1] for section in sections)

        def find(t):
            chunk, low = sections[0][0] + t, sections[0][2]
            before = sections[0][1]
            for begins, number, lower in sections[1:]:
                here = t >= before
                chunk = jnp.where(here, begins + t - before, chunk)
                low = jnp.where(here, lower, low)
                before = before + number
            chunk = jnp.clip(chunk, 0, own * per - 1)
            return pl.multiple_of(chunk * TILE, TILE), low, None

        here = pl.ds(pl.multiple_of(first, TILE), TILE)
        top, den, acc = pipelined(
            total,
            q_t[:, here],
            lambda t: k_n[pl.ds(find(t)[0], TILE), :],
            lambda t: v_t[:, pl.ds(find(t)[0], TILE)],
            find,
            (tops[:, here], dens[:, here], accs[:, here]),
        )
        result = (acc / den).astype(jnp.bfloat16)
        for part in range(TILE // rows):
            out[i * (TILE // rows) + part] = result[:, part * rows : (part + 1) * rows]
        return carry

    lax.fori_loop(0, tokens // TILE, tile, 0)


def attend(lengths, groups, two, q_t, tops, dens, accs):
    n, _, _, rows = two.shape
    tokens = slots = n * rows
    vmem = pl.BlockSpec(memory_space=pltpu.VMEM)
    smem = pl.BlockSpec(memory_space=pltpu.SMEM)
    return pl.pallas_call(
        functools.partial(attend_kernel, tokens, slots),
        out_shape=jax.ShapeDtypeStruct((n, HD, rows), jnp.bfloat16),
        in_specs=[smem, smem] + [vmem] * 5,
        out_specs=vmem,
        scratch_shapes=[
            pltpu.VMEM((slots, HD), jnp.bfloat16),
            pltpu.VMEM((HD, slots), jnp.bfloat16),
        ],
        compiler_params=pltpu.CompilerParams(vmem_limit_bytes=48 << 20),
        name="attend",
    )(lengths, groups, two, q_t, tops, dens, accs)


def project_kernel(n, x, w, out, *scratch):
    landed, w_v, turned, sent, came = scratch[:5]
    send_sem, recv_sem, local_sem, w_sem, over_sem, back_sem = scratch[5:]
    me = lax.axis_index("seq")
    mine = lax.axis_index("head")
    other = 1 - mine
    width, features = w.shape
    half = features // 2
    parts, piece, rows = sent.shape
    loads = []
    for number, side in enumerate((other, mine)):
        at = pl.ds(pl.multiple_of(side * half, half), half)
        loads.append(pltpu.make_async_copy(w.at[:, at], w_v.at[number], w_sem.at[number]))
    greet(me, n, (other,))
    for load in loads:
        load.start()
    greeted(n)
    start, end = exchange(me, n, x, landed, send_sem, recv_sem, local_sem)
    start()
    end()
    turned[...] = landed[...].reshape(width, rows).T

    def share(number, j):
        at = pl.ds(pl.multiple_of(j * piece, piece), piece)
        return jnp.dot(
            turned[...], w_v[number, :, at], preferred_element_type=jnp.float32
        ).T

    def over(j):
        return pltpu.make_async_remote_copy(
            src_ref=sent.at[j],
            dst_ref=came.at[j],
            send_sem=over_sem.at[j],
            recv_sem=back_sem.at[j],
            device_id={"head": other},
            device_id_type=pl.DeviceIdType.MESH,
        )

    def theirs(j, carry):
        sent[j] = share(0, j).astype(jnp.bfloat16)
        over(j).start()
        return carry

    def ours(j, carry):
        part = share(1, j)
        over(j).wait()
        at = pl.ds(pl.multiple_of(j * piece, piece), piece)
        out[at, :] = (part + came[j].astype(jnp.float32)).astype(jnp.bfloat16)
        return carry

    loads[0].wait()
    lax.fori_loop(0, parts, theirs, 0)
    loads[1].wait()
    lax.fori_loop(0, parts, ours, 0)


def project(x, w):
    n, _, rows = x.shape
    width, features = w.shape
    half = features // 2
    parts = half // TILE
    return pl.pallas_call(
        functools.partial(project_kernel, n),
        out_shape=jax.ShapeDtypeStruct((half, rows), x.dtype),
        in_specs=[pl.BlockSpec(memory_space=pltpu.VMEM), pl.BlockSpec(memory_space=pl.ANY)],
        out_specs=pl.BlockSpec(memory_space=pltpu.VMEM),
        scratch_shapes=[
            pltpu.VMEM(x.shape, jnp.bfloat16),
            pltpu.VMEM((2, width, half), jnp.bfloat16),
            pltpu.VMEM((rows, width), jnp.bfloat16),
            pltpu.VMEM((parts, TILE, rows), jnp.bfloat16),
            pltpu.VMEM((parts, TILE, rows), jnp.bfloat16),
            pltpu.SemaphoreType.DMA((n,)),
            pltpu.SemaphoreType.DMA((n,)),
            pltpu.SemaphoreType.DMA,
            pltpu.SemaphoreType.DMA((2,)),
            pltpu.SemaphoreType.DMA((parts,)),
            pltpu.SemaphoreType.DMA((parts,)),
        ],
        compiler_params=pltpu.CompilerParams(
            collective_id=1, has_side_effects=True, vmem_limit_bytes=48 << 20
        ),
        name="project",
    )(x, w)


def by_heads(
    queries, keys, values, cache_k, cache_v, sink_k, sink_v, suffix_lengths, request_group, w_out
):
    n = lax.axis_size("seq")
    me = lax.axis_index("seq")
    sk = lax.dynamic_slice_in_dim(sink_k, me * HD, HD, 1)
    sv = lax.dynamic_slice_in_dim(sink_v, me * HD, HD, 1).T
    two, *state = to_heads(
        n,
        suffix_lengths,
        request_group,
        sk,
        sv,
        queries,
        keys,
        values,
        cache_k,
        cache_v,
    )
    attn = attend(suffix_lengths, request_group, two, *state)
    return project(attn, w_out)


def shards(queries, keys, values, cache_k, *rest):
    n = lax.axis_size("seq")
    rows, width = queries.shape
    fits = (
        n == width // HD
        and n % 4 == 0
        and rows % 128 == 0
        and TILE % rows == 0
        and cache_k.shape[0] == rows
        and (n * rows) % W == 0
        and lax.axis_size("head") == 2
        and rest[-1].shape[1] % (2 * TILE) == 0
    )
    return (by_heads if fits else gathered)(queries, keys, values, cache_k, *rest)


def solution(mesh):
    placed = (
        P("seq", "head"),
        P("seq", "head"),
        P("seq", "head"),
        P("seq", "head"),
        P("seq", "head"),
        P(None, "head"),
        P(None, "head"),
        P(),
        P(),
        P("head", None),
    )
    return jax.shard_map(
        shards, mesh=mesh, in_specs=placed, out_specs=P("head", "seq"), check_vma=False
    )
```

```python
import functools
import math

import jax
import jax.numpy as jnp
from jax import lax
from jax.experimental import pallas as pl
from jax.experimental.pallas import tpu as pltpu
from jax.sharding import PartitionSpec as P

HD = 96
W = 1024
SINKS = 4


def starts_of(lengths):
    place = jnp.arange(lengths.shape[0], dtype=jnp.int32)
    return jnp.sum(jnp.where(place[None, :] < place[:, None], lengths[None, :], 0), axis=1)


def from_behind(array, axis, by):
    devices = lax.axis_size(axis)
    pairs = [(i, i + by) for i in range(devices) if 0 <= i + by < devices]
    return lax.ppermute(array, axis, pairs)


def describe(index, starts, lengths, groups):
    inside = (starts[None, :] <= index[:, None]) & (index[:, None] < (starts + lengths)[None, :])
    flag = inside.astype(jnp.int32)
    found = jnp.sum(flag, axis=1)
    request = jnp.sum(flag * jnp.arange(starts.shape[0], dtype=jnp.int32)[None, :], axis=1)
    request = jnp.where(found > 0, request, -1)
    offset = index - jnp.sum(flag * starts[None, :], axis=1)
    group = jnp.sum(flag * groups[None, :], axis=1)
    return (request, offset, group)


def gathered(
    queries, keys, values, cache_k, cache_v, sink_k, sink_v, suffix_lengths, request_group, w_out
):
    rows, width = queries.shape
    heads = width // HD
    scale = 1.0 / math.sqrt(HD)
    device = lax.axis_index("seq")
    starts = starts_of(suffix_lengths)
    index = device * rows + jnp.arange(rows, dtype=jnp.int32)
    req_q, off_q, grp_q = describe(index, starts, suffix_lengths, request_group)
    q_three = queries.reshape(rows, heads, HD)

    def absorb(state, key_rows, value_rows, mask):
        top, den, acc = state
        count = key_rows.shape[0]
        k_three = key_rows.reshape(count, heads, HD)
        v_three = value_rows.reshape(count, heads, HD)
        score = (
            jnp.einsum("shd,khd->hsk", q_three, k_three, preferred_element_type=jnp.float32) * scale
        )
        score = jnp.where(mask[None], score, jnp.float32(-1e30))
        new_top = jnp.maximum(top, jnp.max(score, axis=2))
        factor = jnp.exp(top - new_top)
        prob = jnp.where(mask[None], jnp.exp(score - new_top[:, :, None]), jnp.float32(0.0))
        den = den * factor + jnp.sum(prob, axis=2)
        part = jnp.einsum(
            "hsk,khd->hsd", prob.astype(jnp.bfloat16), v_three, preferred_element_type=jnp.float32
        )
        acc = acc * factor[:, :, None] + part
        return (new_top, den, acc)

    def suffix_mask(near):
        req_k, off_k, grp_k = describe(near, starts, suffix_lengths, request_group)
        return (
            (req_k[None, :] == req_q[:, None])
            & (near[None, :] <= index[:, None])
            & (index[:, None] - near[None, :] < W)
            & (near[None, :] >= 0)
        )

    state = (
        jnp.full((heads, rows), -1e30, jnp.float32),
        jnp.zeros((heads, rows), jnp.float32),
        jnp.zeros((heads, rows, HD), jnp.float32),
    )
    sink_group = jnp.arange(sink_k.shape[0], dtype=jnp.int32) // SINKS
    state = absorb(state, sink_k, sink_v, grp_q[:, None] == sink_group[None, :])
    pieces = (
        lax.all_gather(cache_k, "seq", axis=0, tiled=True),
        lax.all_gather(cache_v, "seq", axis=0, tiled=True),
    )
    slot = jnp.arange(pieces[0].shape[0], dtype=jnp.int32)
    state = absorb(
        state,
        pieces[0],
        pieces[1],
        (grp_q[:, None] == (slot // W)[None, :]) & ((slot % W)[None, :] > off_q[:, None]),
    )
    state = absorb(state, keys, values, suffix_mask(index))
    reach = W // rows
    current = (keys, values)
    for step in range(1, reach + 1):
        current = from_behind((current[0], current[1]), "seq", 1)
        near = (device - step) * rows + jnp.arange(rows, dtype=jnp.int32)
        state = absorb(state, current[0], current[1], suffix_mask(near))
    top, den, acc = state
    attn = (acc / den[:, :, None]).transpose(1, 0, 2).reshape(rows, width).astype(jnp.bfloat16)
    return lax.psum_scatter(
        jnp.einsum("cd,sc->ds", w_out, attn, preferred_element_type=jnp.float32).astype(
            jnp.bfloat16
        ),
        "head",
        scatter_dimension=0,
        tiled=True,
    )


TILE = 256


def greet(me, n, extra=()):
    barrier = pltpu.get_barrier_semaphore()

    def one(o, carry):
        pl.semaphore_signal(
            barrier,
            inc=1,
            device_id={"seq": lax.rem(me + o, n)},
            device_id_type=pl.DeviceIdType.MESH,
        )
        return carry

    lax.fori_loop(1, n, one, 0)
    for other in extra:
        pl.semaphore_signal(
            barrier, inc=1, device_id={"head": other}, device_id_type=pl.DeviceIdType.MESH
        )


def greeted(count):
    pl.semaphore_wait(pltpu.get_barrier_semaphore(), count)


def exchange(me, n, source, landing, send_sem, recv_sem, local_sem):
    def copy_to(o):
        to = lax.rem(me + o, n)
        return pltpu.make_async_remote_copy(
            src_ref=source.at[to],
            dst_ref=landing.at[me],
            send_sem=send_sem.at[o],
            recv_sem=recv_sem.at[o],
            device_id={"seq": to},
            device_id_type=pl.DeviceIdType.MESH,
        )

    def one_start(o, carry):
        copy_to(o).start()
        return carry

    def one_sent(o, carry):
        copy_to(o).wait_send()
        return carry

    def one_arrived(o, carry):
        copy_to(o).wait_recv()
        return carry

    own = pltpu.make_async_copy(source.at[me], landing.at[me], local_sem)

    def start():
        lax.fori_loop(1, n, one_start, 0)
        own.start()

    def sent():
        lax.fori_loop(1, n, one_sent, 0)

    def arrived():
        lax.fori_loop(1, n, one_arrived, 0)
        own.wait()

    return start, sent, arrived


def pipelined(total, q_tile, key_rows, value_columns, limits, state):
    factor = math.log2(math.e) / math.sqrt(HD)
    column = lax.broadcasted_iota(jnp.int32, (TILE, 1), 0)

    def scores(t):
        return jnp.dot(key_rows(t), q_tile, preferred_element_type=jnp.float32)

    def weigh(t, prob):
        return jnp.dot(value_columns(t), prob, preferred_element_type=jnp.float32)

    def step(t, state):
        top, den, acc, score, prob = state
        following = scores(jnp.minimum(t + 1, total - 1))
        acc = acc + weigh(jnp.maximum(t - 1, 0), prob)
        at, low, high = limits(t)
        index_k = at + column
        seen = index_k > low
        if high is not None:
            seen = seen & (index_k <= high)
        score = jnp.where(seen, score, jnp.float32(-1e30))
        new_top = jnp.maximum(top, jnp.max(score, axis=0, keepdims=True))
        shrink = jnp.exp2((top - new_top) * factor)
        prob = jnp.exp2((score - new_top) * factor)
        den = den * shrink + jnp.sum(prob, axis=0, keepdims=True)
        return new_top, den, acc * shrink, following, prob.astype(jnp.bfloat16)

    state = (*state, scores(0), jnp.zeros((TILE, TILE), jnp.bfloat16))
    top, den, acc, _, prob = lax.fori_loop(0, total, step, state)
    return top, den, acc + weigh(total - 1, prob)


def facts(first, lengths, groups):
    index_q = first + lax.broadcasted_iota(jnp.int32, (1, TILE), 1)
    begin = jnp.int32(0)
    start_q = jnp.zeros((1, TILE), jnp.int32)
    group_q = jnp.zeros((1, TILE), jnp.int32)
    for r in range(lengths.shape[0]):
        inside = index_q >= begin
        start_q = jnp.where(inside, begin, start_q)
        group_q = jnp.where(inside, groups[r], group_q)
        begin = begin + lengths[r]
    return index_q, start_q, group_q


def to_heads_kernel(n, lengths, groups, sk, sv, *refs):
    five, (second, q_t, tops, dens, accs), refs = refs[:5], refs[5:10], refs[10:]
    raw, stage_one, stage_two, first, k_n, v_t, load_sem, send_sem, recv_sem, local_sem = refs
    me = lax.axis_index("seq")
    rows = five[0].shape[0]
    tokens = n * rows
    loads = [pltpu.make_async_copy(five[a], raw.at[a], load_sem.at[a]) for a in range(5)]
    for load in loads:
        load.start()
    greet(me, n)
    ends = []
    for which, (stage, landing, arrays) in enumerate(
        ((stage_one, first, (0, 1, 2)), (stage_two, second, (3, 4)))
    ):
        for place, a in enumerate(arrays):
            loads[a].wait()
            for g in range(n // 4):
                turned = raw[a, :, g * 4 * HD : (g + 1) * 4 * HD].T
                for i in range(4):
                    stage[4 * g + i, place] = turned[i * HD : (i + 1) * HD]
        if which == 0:
            greeted(n - 1)
        else:
            ends[0][0]()
        start, sent, arrived = exchange(
            me, n, stage, landing, send_sem.at[which], recv_sem.at[which], local_sem.at[which]
        )
        start()
        ends.append((sent, arrived))

    ends[0][1]()
    for b in range(n):
        at = pl.ds(b * rows, rows)
        q_t[:, at] = first[b, 0]
        k_n[at, :] = first[b, 1].T
        v_t[:, at] = first[b, 2]
    factor = math.log2(math.e) / math.sqrt(HD)
    sink_column = lax.broadcasted_iota(jnp.int32, (sk.shape[0], 1), 0) // SINKS

    def tile(i, carry):
        here = pl.ds(pl.multiple_of(i * TILE, TILE), TILE)
        index_q, start_q, group_q = facts(i * TILE, lengths, groups)
        q_tile = q_t[:, here]
        score = jnp.dot(sk[...], q_tile, preferred_element_type=jnp.float32)
        score = jnp.where(sink_column == group_q, score, jnp.float32(-1e30))
        top = jnp.max(score, axis=0, keepdims=True)
        prob = jnp.exp2((score - top) * factor)
        den = jnp.sum(prob, axis=0, keepdims=True)
        acc = lax.dot_general(
            sv[...],
            prob.astype(jnp.bfloat16),
            (((0,), (0,)), ((), ())),
            preferred_element_type=jnp.float32,
        )
        begin = jnp.maximum(i - W // TILE, 0)

        def chunk(t):
            return pl.multiple_of((begin + t) * TILE, TILE)

        top, den, acc = pipelined(
            i + 1 - begin,
            q_tile,
            lambda t: k_n[pl.ds(chunk(t), TILE), :],
            lambda t: v_t[:, pl.ds(chunk(t), TILE)],
            lambda t: (chunk(t), start_q - 1, index_q),
            (top, den, acc),
        )
        tops[:, here] = top
        dens[:, here] = den
        accs[:, here] = acc
        return carry

    lax.fori_loop(0, tokens // TILE, tile, 0)
    ends[1][0]()
    ends[1][1]()


def to_heads(n, lengths, groups, sk, sv, *arrays):
    rows, width = arrays[0].shape
    tokens = n * rows
    shapes = [(n, 3, HD, rows), (n, 2, HD, rows)]
    anywhere = pl.BlockSpec(memory_space=pl.ANY)
    vmem = pl.BlockSpec(memory_space=pltpu.VMEM)
    smem = pl.BlockSpec(memory_space=pltpu.SMEM)
    return pl.pallas_call(
        functools.partial(to_heads_kernel, n),
        out_shape=[
            jax.ShapeDtypeStruct(shapes[1], jnp.bfloat16),
            jax.ShapeDtypeStruct((HD, tokens), jnp.bfloat16),
            jax.ShapeDtypeStruct((1, tokens), jnp.float32),
            jax.ShapeDtypeStruct((1, tokens), jnp.float32),
            jax.ShapeDtypeStruct((HD, tokens), jnp.float32),
        ],
        in_specs=[smem, smem, vmem, vmem] + [anywhere] * 5,
        out_specs=[anywhere] + [vmem] * 4,
        scratch_shapes=[
            pltpu.VMEM((5, rows, width), jnp.bfloat16),
            pltpu.VMEM(shapes[0], jnp.bfloat16),
            pltpu.VMEM(shapes[1], jnp.bfloat16),
            pltpu.VMEM(shapes[0], jnp.bfloat16),
            pltpu.VMEM((tokens, HD), jnp.bfloat16),
            pltpu.VMEM((HD, tokens), jnp.bfloat16),
            pltpu.SemaphoreType.DMA((5,)),
            pltpu.SemaphoreType.DMA((2, n)),
            pltpu.SemaphoreType.DMA((2, n)),
            pltpu.SemaphoreType.DMA((2,)),
        ],
        compiler_params=pltpu.CompilerParams(
            collective_id=0, has_side_effects=True, vmem_limit_bytes=62 << 20
        ),
        name="to_heads",
    )(lengths, groups, sk, sv, *arrays)


def attend_kernel(tokens, slots, lengths, groups, two, q_t, tops, dens, accs, out, k_n, v_t):
    n, _, _, rows = two.shape
    own = slots // W
    per = W // TILE
    for b in range(n):
        at = pl.ds(b * rows, rows)
        k_n[at, :] = two[b, 0].T
        v_t[:, at] = two[b, 1]

    def tile(i, carry):
        first = i * TILE
        last = first + TILE
        index_q, start_q, group_q = facts(first, lengths, groups)
        begin = jnp.int32(0)
        lowest = [jnp.int32(W - 1) for _ in range(own)]
        for r in range(lengths.shape[0]):
            end = begin + lengths[r]
            low = jnp.maximum(first, begin)
            touches = low < jnp.minimum(last, end)
            for g in range(own):
                lowest[g] = jnp.where(
                    touches & (groups[r] == g), jnp.minimum(lowest[g], low - begin), lowest[g]
                )
            begin = end
        offset_q = index_q - start_q
        sections = []
        for g in range(own):
            chunk = (lowest[g] + 1) // TILE
            limit = g * W + jnp.where(group_q == g, offset_q, jnp.int32(W))
            sections.append((g * per + chunk, per - chunk, limit))
        total = sum(section[1] for section in sections)

        def find(t):
            chunk, low = sections[0][0] + t, sections[0][2]
            before = sections[0][1]
            for begins, number, lower in sections[1:]:
                here = t >= before
                chunk = jnp.where(here, begins + t - before, chunk)
                low = jnp.where(here, lower, low)
                before = before + number
            chunk = jnp.clip(chunk, 0, own * per - 1)
            return pl.multiple_of(chunk * TILE, TILE), low, None

        here = pl.ds(pl.multiple_of(first, TILE), TILE)
        top, den, acc = pipelined(
            total,
            q_t[:, here],
            lambda t: k_n[pl.ds(find(t)[0], TILE), :],
            lambda t: v_t[:, pl.ds(find(t)[0], TILE)],
            find,
            (tops[:, here], dens[:, here], accs[:, here]),
        )
        result = (acc / den).astype(jnp.bfloat16)
        for part in range(TILE // rows):
            out[i * (TILE // rows) + part] = result[:, part * rows : (part + 1) * rows]
        return carry

    lax.fori_loop(0, tokens // TILE, tile, 0)


def attend(lengths, groups, two, q_t, tops, dens, accs):
    n, _, _, rows = two.shape
    tokens = slots = n * rows
    vmem = pl.BlockSpec(memory_space=pltpu.VMEM)
    smem = pl.BlockSpec(memory_space=pltpu.SMEM)
    return pl.pallas_call(
        functools.partial(attend_kernel, tokens, slots),
        out_shape=jax.ShapeDtypeStruct((n, HD, rows), jnp.bfloat16),
        in_specs=[smem, smem] + [vmem] * 5,
        out_specs=vmem,
        scratch_shapes=[
            pltpu.VMEM((slots, HD), jnp.bfloat16),
            pltpu.VMEM((HD, slots), jnp.bfloat16),
        ],
        compiler_params=pltpu.CompilerParams(vmem_limit_bytes=62 << 20),
        name="attend",
    )(lengths, groups, two, q_t, tops, dens, accs)


def project_kernel(n, x, w, out, *scratch):
    landed, w_v, turned, sent, came = scratch[:5]
    send_sem, recv_sem, local_sem, w_sem, over_sem, back_sem = scratch[5:]
    me = lax.axis_index("seq")
    mine = lax.axis_index("head")
    other = 1 - mine
    width, features = w.shape
    half = features // 2
    parts, piece, rows = sent.shape
    loads = []
    for number, side in enumerate((other, mine)):
        at = pl.ds(pl.multiple_of(side * half, half), half)
        loads.append(pltpu.make_async_copy(w.at[:, at], w_v.at[number], w_sem.at[number]))
    greet(me, n, (other,))
    for load in loads:
        load.start()
    greeted(n)
    start, all_sent, arrived = exchange(me, n, x, landed, send_sem, recv_sem, local_sem)
    start()
    arrived()
    turned[...] = landed[...].reshape(width, rows).T

    def share(number, j):
        at = pl.ds(pl.multiple_of(j * piece, piece), piece)
        return jnp.dot(
            turned[...], w_v[number, :, at], preferred_element_type=jnp.float32
        ).T

    def over(j):
        return pltpu.make_async_remote_copy(
            src_ref=sent.at[j],
            dst_ref=came.at[j],
            send_sem=over_sem.at[j],
            recv_sem=back_sem.at[j],
            device_id={"head": other},
            device_id_type=pl.DeviceIdType.MESH,
        )

    def theirs(j, carry):
        sent[j] = share(0, j).astype(jnp.bfloat16)
        over(j).start()
        return carry

    def ours(j, carry):
        part = share(1, j)
        over(j).wait()
        at = pl.ds(pl.multiple_of(j * piece, piece), piece)
        out[at, :] = (part + came[j].astype(jnp.float32)).astype(jnp.bfloat16)
        return carry

    loads[0].wait()
    lax.fori_loop(0, parts, theirs, 0)
    loads[1].wait()
    lax.fori_loop(0, parts, ours, 0)
    all_sent()


def project(x, w):
    n, _, rows = x.shape
    width, features = w.shape
    half = features // 2
    parts = half // TILE
    return pl.pallas_call(
        functools.partial(project_kernel, n),
        out_shape=jax.ShapeDtypeStruct((half, rows), x.dtype),
        in_specs=[pl.BlockSpec(memory_space=pltpu.VMEM), pl.BlockSpec(memory_space=pl.ANY)],
        out_specs=pl.BlockSpec(memory_space=pltpu.VMEM),
        scratch_shapes=[
            pltpu.VMEM(x.shape, jnp.bfloat16),
            pltpu.VMEM((2, width, half), jnp.bfloat16),
            pltpu.VMEM((rows, width), jnp.bfloat16),
            pltpu.VMEM((parts, TILE, rows), jnp.bfloat16),
            pltpu.VMEM((parts, TILE, rows), jnp.bfloat16),
            pltpu.SemaphoreType.DMA((n,)),
            pltpu.SemaphoreType.DMA((n,)),
            pltpu.SemaphoreType.DMA,
            pltpu.SemaphoreType.DMA((2,)),
            pltpu.SemaphoreType.DMA((parts,)),
            pltpu.SemaphoreType.DMA((parts,)),
        ],
        compiler_params=pltpu.CompilerParams(
            collective_id=1, has_side_effects=True, vmem_limit_bytes=62 << 20
        ),
        name="project",
    )(x, w)


def by_heads(
    queries, keys, values, cache_k, cache_v, sink_k, sink_v, suffix_lengths, request_group, w_out
):
    n = lax.axis_size("seq")
    me = lax.axis_index("seq")
    sk = lax.dynamic_slice_in_dim(sink_k, me * HD, HD, 1)
    sv = lax.dynamic_slice_in_dim(sink_v, me * HD, HD, 1)
    two, *state = to_heads(
        n,
        suffix_lengths,
        request_group,
        sk,
        sv,
        queries,
        keys,
        values,
        cache_k,
        cache_v,
    )
    attn = attend(suffix_lengths, request_group, two, *state)
    return project(attn, w_out)


def shards(queries, keys, values, cache_k, *rest):
    n = lax.axis_size("seq")
    rows, width = queries.shape
    fits = (
        n == width // HD
        and n % 4 == 0
        and rows % 128 == 0
        and TILE % rows == 0
        and cache_k.shape[0] == rows
        and (n * rows) % W == 0
        and lax.axis_size("head") == 2
        and rest[-1].shape[1] % (2 * TILE) == 0
    )
    return (by_heads if fits else gathered)(queries, keys, values, cache_k, *rest)


def solution(mesh):
    placed = (
        P("seq", "head"),
        P("seq", "head"),
        P("seq", "head"),
        P("seq", "head"),
        P("seq", "head"),
        P(None, "head"),
        P(None, "head"),
        P(),
        P(),
        P("head", None),
    )
    return jax.shard_map(
        shards, mesh=mesh, in_specs=placed, out_specs=P("head", "seq"), check_vma=False
    )
```

```python
import functools
import math

import jax
import jax.numpy as jnp
from jax import lax
from jax.experimental import pallas as pl
from jax.experimental.pallas import tpu as pltpu
from jax.sharding import PartitionSpec as P

HD = 96
W = 1024
SINKS = 4


def starts_of(lengths):
    place = jnp.arange(lengths.shape[0], dtype=jnp.int32)
    return jnp.sum(jnp.where(place[None, :] < place[:, None], lengths[None, :], 0), axis=1)


def from_behind(array, axis, by):
    devices = lax.axis_size(axis)
    pairs = [(i, i + by) for i in range(devices) if 0 <= i + by < devices]
    return lax.ppermute(array, axis, pairs)


def describe(index, starts, lengths, groups):
    inside = (starts[None, :] <= index[:, None]) & (index[:, None] < (starts + lengths)[None, :])
    flag = inside.astype(jnp.int32)
    found = jnp.sum(flag, axis=1)
    request = jnp.sum(flag * jnp.arange(starts.shape[0], dtype=jnp.int32)[None, :], axis=1)
    request = jnp.where(found > 0, request, -1)
    offset = index - jnp.sum(flag * starts[None, :], axis=1)
    group = jnp.sum(flag * groups[None, :], axis=1)
    return (request, offset, group)


def gathered(
    queries, keys, values, cache_k, cache_v, sink_k, sink_v, suffix_lengths, request_group, w_out
):
    rows, width = queries.shape
    heads = width // HD
    scale = 1.0 / math.sqrt(HD)
    device = lax.axis_index("seq")
    starts = starts_of(suffix_lengths)
    index = device * rows + jnp.arange(rows, dtype=jnp.int32)
    req_q, off_q, grp_q = describe(index, starts, suffix_lengths, request_group)
    q_three = queries.reshape(rows, heads, HD)

    def absorb(state, key_rows, value_rows, mask):
        top, den, acc = state
        count = key_rows.shape[0]
        k_three = key_rows.reshape(count, heads, HD)
        v_three = value_rows.reshape(count, heads, HD)
        score = (
            jnp.einsum("shd,khd->hsk", q_three, k_three, preferred_element_type=jnp.float32) * scale
        )
        score = jnp.where(mask[None], score, jnp.float32(-1e30))
        new_top = jnp.maximum(top, jnp.max(score, axis=2))
        factor = jnp.exp(top - new_top)
        prob = jnp.where(mask[None], jnp.exp(score - new_top[:, :, None]), jnp.float32(0.0))
        den = den * factor + jnp.sum(prob, axis=2)
        part = jnp.einsum(
            "hsk,khd->hsd", prob.astype(jnp.bfloat16), v_three, preferred_element_type=jnp.float32
        )
        acc = acc * factor[:, :, None] + part
        return (new_top, den, acc)

    def suffix_mask(near):
        req_k, off_k, grp_k = describe(near, starts, suffix_lengths, request_group)
        return (
            (req_k[None, :] == req_q[:, None])
            & (near[None, :] <= index[:, None])
            & (index[:, None] - near[None, :] < W)
            & (near[None, :] >= 0)
        )

    state = (
        jnp.full((heads, rows), -1e30, jnp.float32),
        jnp.zeros((heads, rows), jnp.float32),
        jnp.zeros((heads, rows, HD), jnp.float32),
    )
    sink_group = jnp.arange(sink_k.shape[0], dtype=jnp.int32) // SINKS
    state = absorb(state, sink_k, sink_v, grp_q[:, None] == sink_group[None, :])
    pieces = (
        lax.all_gather(cache_k, "seq", axis=0, tiled=True),
        lax.all_gather(cache_v, "seq", axis=0, tiled=True),
    )
    slot = jnp.arange(pieces[0].shape[0], dtype=jnp.int32)
    state = absorb(
        state,
        pieces[0],
        pieces[1],
        (grp_q[:, None] == (slot // W)[None, :]) & ((slot % W)[None, :] > off_q[:, None]),
    )
    state = absorb(state, keys, values, suffix_mask(index))
    reach = W // rows
    current = (keys, values)
    for step in range(1, reach + 1):
        current = from_behind((current[0], current[1]), "seq", 1)
        near = (device - step) * rows + jnp.arange(rows, dtype=jnp.int32)
        state = absorb(state, current[0], current[1], suffix_mask(near))
    top, den, acc = state
    attn = (acc / den[:, :, None]).transpose(1, 0, 2).reshape(rows, width).astype(jnp.bfloat16)
    return lax.psum_scatter(
        jnp.einsum("cd,sc->ds", w_out, attn, preferred_element_type=jnp.float32).astype(
            jnp.bfloat16
        ),
        "head",
        scatter_dimension=0,
        tiled=True,
    )


TILE = 256


def greet(me, n, extra=()):
    barrier = pltpu.get_barrier_semaphore()

    def one(o, carry):
        pl.semaphore_signal(
            barrier,
            inc=1,
            device_id={"seq": lax.rem(me + o, n)},
            device_id_type=pl.DeviceIdType.MESH,
        )
        return carry

    lax.fori_loop(1, n, one, 0)
    for other in extra:
        pl.semaphore_signal(
            barrier, inc=1, device_id={"head": other}, device_id_type=pl.DeviceIdType.MESH
        )


def greeted(count):
    pl.semaphore_wait(pltpu.get_barrier_semaphore(), count)


def exchange(me, n, source, landing, send_sem, recv_sem, local_sem):
    def copy_to(o):
        to = lax.rem(me + o, n)
        return pltpu.make_async_remote_copy(
            src_ref=source.at[to],
            dst_ref=landing.at[me],
            send_sem=send_sem.at[o],
            recv_sem=recv_sem.at[o],
            device_id={"seq": to},
            device_id_type=pl.DeviceIdType.MESH,
        )

    def one_start(k, carry):
        copy_to(n // 2 + (k + 1) // 2 * (1 - 2 * (k % 2))).start()
        return carry

    def one_sent(o, carry):
        copy_to(o).wait_send()
        return carry

    def one_arrived(o, carry):
        copy_to(o).wait_recv()
        return carry

    own = pltpu.make_async_copy(source.at[me], landing.at[me], local_sem)

    def start():
        lax.fori_loop(0, n - 1, one_start, 0)
        own.start()

    def sent():
        lax.fori_loop(1, n, one_sent, 0)

    def arrived():
        lax.fori_loop(1, n, one_arrived, 0)
        own.wait()

    return start, sent, arrived


def pipelined(total, q_tile, key_rows, value_columns, limits, state):
    factor = math.log2(math.e) / math.sqrt(HD)
    column = lax.broadcasted_iota(jnp.int32, (TILE, 1), 0)

    def scores(t):
        return jnp.dot(key_rows(t), q_tile, preferred_element_type=jnp.float32)

    def weigh(t, prob):
        return jnp.dot(value_columns(t), prob, preferred_element_type=jnp.float32)

    def step(t, state):
        top, den, acc, score, prob = state
        following = scores(jnp.minimum(t + 1, total - 1))
        acc = acc + weigh(jnp.maximum(t - 1, 0), prob)
        at, low, high = limits(t)
        index_k = at + column
        seen = index_k > low
        if high is not None:
            seen = seen & (index_k <= high)
        score = jnp.where(seen, score, jnp.float32(-1e30))
        new_top = jnp.maximum(top, jnp.max(score, axis=0, keepdims=True))
        shrink = jnp.exp2((top - new_top) * factor)
        prob = jnp.exp2((score - new_top) * factor)
        den = den * shrink + jnp.sum(prob, axis=0, keepdims=True)
        return new_top, den, acc * shrink, following, prob.astype(jnp.bfloat16)

    state = (*state, scores(0), jnp.zeros((TILE, TILE), jnp.bfloat16))
    top, den, acc, _, prob = lax.fori_loop(0, total, step, state)
    return top, den, acc + weigh(total - 1, prob)


def facts(first, lengths, groups):
    index_q = first + lax.broadcasted_iota(jnp.int32, (1, TILE), 1)
    begin = jnp.int32(0)
    start_q = jnp.zeros((1, TILE), jnp.int32)
    group_q = jnp.zeros((1, TILE), jnp.int32)
    for r in range(lengths.shape[0]):
        inside = index_q >= begin
        start_q = jnp.where(inside, begin, start_q)
        group_q = jnp.where(inside, groups[r], group_q)
        begin = begin + lengths[r]
    return index_q, start_q, group_q


def to_heads_kernel(n, lengths, groups, sk, sv, *refs):
    five, (second, q_t, tops, dens, accs), refs = refs[:5], refs[5:10], refs[10:]
    raw, stage_one, stage_two, first, k_n, v_t, load_sem, send_sem, recv_sem, local_sem = refs
    me = lax.axis_index("seq")
    rows = five[0].shape[0]
    tokens = n * rows
    loads = [pltpu.make_async_copy(five[a], raw.at[a], load_sem.at[a]) for a in range(5)]
    for load in loads:
        load.start()
    greet(me, n)
    ends = []
    for which, (stage, landing, arrays) in enumerate(
        ((stage_one, first, (0, 1, 2)), (stage_two, second, (3, 4)))
    ):
        for place, a in enumerate(arrays):
            loads[a].wait()
            for g in range(n // 4):
                turned = raw[a, :, g * 4 * HD : (g + 1) * 4 * HD].T
                for i in range(4):
                    stage[4 * g + i, place] = turned[i * HD : (i + 1) * HD]
        if which == 0:
            greeted(n - 1)
        else:
            ends[0][0]()
        start, sent, arrived = exchange(
            me, n, stage, landing, send_sem.at[which], recv_sem.at[which], local_sem.at[which]
        )
        start()
        ends.append((sent, arrived))

    ends[0][1]()
    for b in range(n):
        at = pl.ds(b * rows, rows)
        q_t[:, at] = first[b, 0]
        k_n[at, :] = first[b, 1].T
        v_t[:, at] = first[b, 2]
    factor = math.log2(math.e) / math.sqrt(HD)
    sink_column = lax.broadcasted_iota(jnp.int32, (sk.shape[0], 1), 0) // SINKS

    def tile(i, carry):
        here = pl.ds(pl.multiple_of(i * TILE, TILE), TILE)
        index_q, start_q, group_q = facts(i * TILE, lengths, groups)
        q_tile = q_t[:, here]
        score = jnp.dot(sk[...], q_tile, preferred_element_type=jnp.float32)
        score = jnp.where(sink_column == group_q, score, jnp.float32(-1e30))
        top = jnp.max(score, axis=0, keepdims=True)
        prob = jnp.exp2((score - top) * factor)
        den = jnp.sum(prob, axis=0, keepdims=True)
        acc = lax.dot_general(
            sv[...],
            prob.astype(jnp.bfloat16),
            (((0,), (0,)), ((), ())),
            preferred_element_type=jnp.float32,
        )
        begin = jnp.maximum(i - W // TILE, 0)

        def chunk(t):
            return pl.multiple_of((begin + t) * TILE, TILE)

        top, den, acc = pipelined(
            i + 1 - begin,
            q_tile,
            lambda t: k_n[pl.ds(chunk(t), TILE), :],
            lambda t: v_t[:, pl.ds(chunk(t), TILE)],
            lambda t: (chunk(t), start_q - 1, index_q),
            (top, den, acc),
        )
        tops[:, here] = top
        dens[:, here] = den
        accs[:, here] = acc
        return carry

    lax.fori_loop(0, tokens // TILE, tile, 0)
    ends[1][0]()
    ends[1][1]()


def to_heads(n, lengths, groups, sk, sv, *arrays):
    rows, width = arrays[0].shape
    tokens = n * rows
    shapes = [(n, 3, HD, rows), (n, 2, HD, rows)]
    anywhere = pl.BlockSpec(memory_space=pl.ANY)
    vmem = pl.BlockSpec(memory_space=pltpu.VMEM)
    smem = pl.BlockSpec(memory_space=pltpu.SMEM)
    return pl.pallas_call(
        functools.partial(to_heads_kernel, n),
        out_shape=[
            jax.ShapeDtypeStruct(shapes[1], jnp.bfloat16),
            jax.ShapeDtypeStruct((HD, tokens), jnp.bfloat16),
            jax.ShapeDtypeStruct((1, tokens), jnp.float32),
            jax.ShapeDtypeStruct((1, tokens), jnp.float32),
            jax.ShapeDtypeStruct((HD, tokens), jnp.float32),
        ],
        in_specs=[smem, smem, vmem, vmem] + [anywhere] * 5,
        out_specs=[anywhere] + [vmem] * 4,
        scratch_shapes=[
            pltpu.VMEM((5, rows, width), jnp.bfloat16),
            pltpu.VMEM(shapes[0], jnp.bfloat16),
            pltpu.VMEM(shapes[1], jnp.bfloat16),
            pltpu.VMEM(shapes[0], jnp.bfloat16),
            pltpu.VMEM((tokens, HD), jnp.bfloat16),
            pltpu.VMEM((HD, tokens), jnp.bfloat16),
            pltpu.SemaphoreType.DMA((5,)),
            pltpu.SemaphoreType.DMA((2, n)),
            pltpu.SemaphoreType.DMA((2, n)),
            pltpu.SemaphoreType.DMA((2,)),
        ],
        compiler_params=pltpu.CompilerParams(
            collective_id=0, has_side_effects=True, vmem_limit_bytes=62 << 20
        ),
        name="to_heads",
    )(lengths, groups, sk, sv, *arrays)


def attend_kernel(tokens, slots, lengths, groups, two, q_t, tops, dens, accs, out, k_n, v_t):
    n, _, _, rows = two.shape
    own = slots // W
    per = W // TILE
    for b in range(n):
        at = pl.ds(b * rows, rows)
        k_n[at, :] = two[b, 0].T
        v_t[:, at] = two[b, 1]

    def tile(i, carry):
        first = i * TILE
        last = first + TILE
        index_q, start_q, group_q = facts(first, lengths, groups)
        begin = jnp.int32(0)
        lowest = [jnp.int32(W - 1) for _ in range(own)]
        for r in range(lengths.shape[0]):
            end = begin + lengths[r]
            low = jnp.maximum(first, begin)
            touches = low < jnp.minimum(last, end)
            for g in range(own):
                lowest[g] = jnp.where(
                    touches & (groups[r] == g), jnp.minimum(lowest[g], low - begin), lowest[g]
                )
            begin = end
        offset_q = index_q - start_q
        sections = []
        for g in range(own):
            chunk = (lowest[g] + 1) // TILE
            limit = g * W + jnp.where(group_q == g, offset_q, jnp.int32(W))
            sections.append((g * per + chunk, per - chunk, limit))
        total = sum(section[1] for section in sections)

        def find(t):
            chunk, low = sections[0][0] + t, sections[0][2]
            before = sections[0][1]
            for begins, number, lower in sections[1:]:
                here = t >= before
                chunk = jnp.where(here, begins + t - before, chunk)
                low = jnp.where(here, lower, low)
                before = before + number
            chunk = jnp.clip(chunk, 0, own * per - 1)
            return pl.multiple_of(chunk * TILE, TILE), low, None

        here = pl.ds(pl.multiple_of(first, TILE), TILE)
        top, den, acc = pipelined(
            total,
            q_t[:, here],
            lambda t: k_n[pl.ds(find(t)[0], TILE), :],
            lambda t: v_t[:, pl.ds(find(t)[0], TILE)],
            find,
            (tops[:, here], dens[:, here], accs[:, here]),
        )
        result = (acc / den).astype(jnp.bfloat16)
        for part in range(TILE // rows):
            out[i * (TILE // rows) + part] = result[:, part * rows : (part + 1) * rows]
        return carry

    lax.fori_loop(0, tokens // TILE, tile, 0)


def attend(lengths, groups, two, q_t, tops, dens, accs):
    n, _, _, rows = two.shape
    tokens = slots = n * rows
    vmem = pl.BlockSpec(memory_space=pltpu.VMEM)
    smem = pl.BlockSpec(memory_space=pltpu.SMEM)
    return pl.pallas_call(
        functools.partial(attend_kernel, tokens, slots),
        out_shape=jax.ShapeDtypeStruct((n, HD, rows), jnp.bfloat16),
        in_specs=[smem, smem] + [vmem] * 5,
        out_specs=vmem,
        scratch_shapes=[
            pltpu.VMEM((slots, HD), jnp.bfloat16),
            pltpu.VMEM((HD, slots), jnp.bfloat16),
        ],
        compiler_params=pltpu.CompilerParams(vmem_limit_bytes=62 << 20),
        name="attend",
    )(lengths, groups, two, q_t, tops, dens, accs)


def project_kernel(n, x, w, out, *scratch):
    landed, w_v, turned, sent, came = scratch[:5]
    send_sem, recv_sem, local_sem, w_sem, over_sem, back_sem = scratch[5:]
    me = lax.axis_index("seq")
    mine = lax.axis_index("head")
    other = 1 - mine
    width, features = w.shape
    half = features // 2
    parts, piece, rows = sent.shape
    loads = []
    for number, side in enumerate((other, mine)):
        at = pl.ds(pl.multiple_of(side * half, half), half)
        loads.append(pltpu.make_async_copy(w.at[:, at], w_v.at[number], w_sem.at[number]))
    greet(me, n, (other,))
    for load in loads:
        load.start()
    greeted(n)
    start, all_sent, arrived = exchange(me, n, x, landed, send_sem, recv_sem, local_sem)
    start()
    arrived()
    turned[...] = landed[...].reshape(width, rows).T

    def share(number, j):
        at = pl.ds(pl.multiple_of(j * piece, piece), piece)
        return jnp.dot(
            turned[...], w_v[number, :, at], preferred_element_type=jnp.float32
        ).T

    def over(j):
        return pltpu.make_async_remote_copy(
            src_ref=sent.at[j],
            dst_ref=came.at[j],
            send_sem=over_sem.at[j],
            recv_sem=back_sem.at[j],
            device_id={"head": other},
            device_id_type=pl.DeviceIdType.MESH,
        )

    def theirs(j, carry):
        sent[j] = share(0, j).astype(jnp.bfloat16)
        over(j).start()
        return carry

    def ours(j, carry):
        part = share(1, j)
        over(j).wait()
        at = pl.ds(pl.multiple_of(j * piece, piece), piece)
        out[at, :] = (part + came[j].astype(jnp.float32)).astype(jnp.bfloat16)
        return carry

    loads[0].wait()
    lax.fori_loop(0, parts, theirs, 0)
    loads[1].wait()
    lax.fori_loop(0, parts, ours, 0)
    all_sent()


def project(x, w):
    n, _, rows = x.shape
    width, features = w.shape
    half = features // 2
    parts = half // TILE
    return pl.pallas_call(
        functools.partial(project_kernel, n),
        out_shape=jax.ShapeDtypeStruct((half, rows), x.dtype),
        in_specs=[pl.BlockSpec(memory_space=pltpu.VMEM), pl.BlockSpec(memory_space=pl.ANY)],
        out_specs=pl.BlockSpec(memory_space=pltpu.VMEM),
        scratch_shapes=[
            pltpu.VMEM(x.shape, jnp.bfloat16),
            pltpu.VMEM((2, width, half), jnp.bfloat16),
            pltpu.VMEM((rows, width), jnp.bfloat16),
            pltpu.VMEM((parts, TILE, rows), jnp.bfloat16),
            pltpu.VMEM((parts, TILE, rows), jnp.bfloat16),
            pltpu.SemaphoreType.DMA((n,)),
            pltpu.SemaphoreType.DMA((n,)),
            pltpu.SemaphoreType.DMA,
            pltpu.SemaphoreType.DMA((2,)),
            pltpu.SemaphoreType.DMA((parts,)),
            pltpu.SemaphoreType.DMA((parts,)),
        ],
        compiler_params=pltpu.CompilerParams(
            collective_id=1, has_side_effects=True, vmem_limit_bytes=48 << 20
        ),
        name="project",
    )(x, w)


def by_heads(
    queries, keys, values, cache_k, cache_v, sink_k, sink_v, suffix_lengths, request_group, w_out
):
    n = lax.axis_size("seq")
    me = lax.axis_index("seq")
    sk = lax.dynamic_slice_in_dim(sink_k, me * HD, HD, 1)
    sv = lax.dynamic_slice_in_dim(sink_v, me * HD, HD, 1)
    two, *state = to_heads(
        n,
        suffix_lengths,
        request_group,
        sk,
        sv,
        queries,
        keys,
        values,
        cache_k,
        cache_v,
    )
    attn = attend(suffix_lengths, request_group, two, *state)
    return project(attn, w_out)


def shards(queries, keys, values, cache_k, *rest):
    n = lax.axis_size("seq")
    rows, width = queries.shape
    fits = (
        n == width // HD
        and n % 4 == 0
        and rows % 128 == 0
        and TILE % rows == 0
        and cache_k.shape[0] == rows
        and (n * rows) % W == 0
        and lax.axis_size("head") == 2
        and rest[-1].shape[1] % (2 * TILE) == 0
    )
    return (by_heads if fits else gathered)(queries, keys, values, cache_k, *rest)


def solution(mesh):
    placed = (
        P("seq", "head"),
        P("seq", "head"),
        P("seq", "head"),
        P("seq", "head"),
        P("seq", "head"),
        P(None, "head"),
        P(None, "head"),
        P(),
        P(),
        P("head", None),
    )
    return jax.shard_map(
        shards, mesh=mesh, in_specs=placed, out_specs=P("head", "seq"), check_vma=False
    )
```
